128 devices in a mesh: tensor: 8 (over z_lo, x), decode: 16 (over z_hi, y, core).
Axes of the slice: x: 4, y: 4, z: 4 (z_hi: 2, z_lo: 2; z = z_hi * 2 + z_lo), core: 2. Of those that a mesh axis runs over, the one named last changes fastest.
Arguments:
- hidden_in: bfloat16 [16, 512, 8192], P('decode', 'tensor'), may hold values from -640 to 640
- norm_gain: float32 [8192], replicated, may hold values from 0.5 to 2
- w_query: bfloat16 [8192, 4096], P('decode', 'tensor'), may hold values from -0.0625 to 0.0625
- w_key: bfloat16 [8192, 1024], P('decode', 'tensor'), may hold values from -0.0625 to 0.0625
- w_value: bfloat16 [8192, 1024], P('decode', 'tensor'), may hold values from -0.0625 to 0.0625
- w_out: bfloat16 [4096, 8192], P('tensor', 'decode'), may hold values from -3 to 3
- cache_k: bfloat16 [16, 8, 8192, 128], P('decode', 'tensor'), may hold values from -128 to 128
- cache_v: bfloat16 [16, 8, 8192, 128], P('decode', 'tensor'), may hold values from -6 to 6
- prefix_len: int32 [16], P('decode'), may hold values from 2048 to 8192, as said below
- page_owner: int32 [16, 4], P('decode'), may hold values from 0 to 15, as said below
Outputs:
- attn_out: bfloat16 [16, 512, 8192], P('decode', 'tensor')
- owned_pages: bfloat16 [16, 32, 2, 128, 1024], P('decode', None, None, None, 'tensor')
- owned_scales: bfloat16 [16, 32, 2, 8], P('decode', None, None, 'tensor')
- owned_ids: int32 [16, 32], P('decode')
The draws below stay inside these ranges and needn't reach their ends.
Inputs may be any that keep to these rules, and one draw needn't show every extreme that they name: `prefix_len`: one prompt has 8192 live positions and another 8192 // 4. `page_owner`: no prompt sends more than 2 pages to one owner, and some prompt sends exactly 2 pages to some owner.
All inputs are finite; a program needn't handle non-finite values.
Results may differ from the reference program's by a relative error of at most 0.02.
Values may be sent and summed in bfloat16 or wider, within the bound.
No kernel may reach another device: no remote copies, remote signals or barrier semaphores. Data moves between devices by JAX's collectives and lax.ppermute only.
A program may use at most 192 MiB of HBM per device.

```python
import math
import jax
import jax.numpy as jnp
from jax import lax

D = 8192
HD = 128
QPK = 4
PREFIX = 8192
PAGE = 128
CAP = 2
KV_HEADS = 8
HEADS = 32
SPAN = 512
PAGES = 4
N_DECODE = 16


def draw_hidden_in(key, part):
    key = jax.random.fold_in(key, 11)
    base_key, row_key, col_key = jax.random.split(key, 3)
    shape = (N_DECODE, SPAN, D)
    base = jnp.clip(jax.random.normal(base_key, shape, jnp.float32), -6.0, 6.0)
    row_top = math.log(10.0)
    row_scale = jnp.exp(jax.random.uniform(row_key, (N_DECODE, SPAN, 1), jnp.float32, 0.0, row_top))
    col_scale = jnp.exp(jax.random.uniform(col_key, (1, 1, D), jnp.float32, 0.0, math.log(10.0)))
    return (base * row_scale * col_scale).astype(jnp.bfloat16)


def draw_cache_k(key, part):
    key = jax.random.fold_in(key, 23)
    base_key = jax.random.fold_in(key, 0)
    shape = (N_DECODE, KV_HEADS, PREFIX, HD)
    base = jnp.clip(jax.random.normal(base_key, shape, jnp.float32), -6.0, 6.0)
    return base.astype(jnp.bfloat16)


def draw_prefix_len(key, part):
    key = jax.random.fold_in(key, 37)
    len_key, long_key, short_key = jax.random.split(key, 3)
    lengths = jax.random.randint(len_key, (N_DECODE,), PREFIX // 4, PREFIX + 1)
    longest = jax.random.randint(long_key, (), 0, N_DECODE)
    shortest = (longest + 1 + jax.random.randint(short_key, (), 0, N_DECODE - 1)) % N_DECODE
    place = jnp.arange(N_DECODE, dtype=jnp.int32)
    lengths = jnp.where(place == longest, PREFIX, lengths)
    lengths = jnp.where(place == shortest, PREFIX // 4, lengths)
    return lengths.astype(jnp.int32)


def shuffle_pages(one_key):
    return jax.random.permutation(one_key, PAGES)


def shuffle_slots(one_key):
    return jax.random.permutation(one_key, (N_DECODE - 1) * CAP)


def shuffle_every(one_key):
    return jax.random.permutation(one_key, N_DECODE * CAP)


def place_owners(order, by_position):
    return jnp.zeros((PAGES,), jnp.int32).at[order].set(by_position)


def draw_page_owner(key, part):
    key = jax.random.fold_in(key, 53)
    busy_key, order_key, slot_key, prompt_key, every_key = jax.random.split(key, 5)
    busy = jax.random.randint(busy_key, (), 0, N_DECODE)
    chosen = jax.random.randint(prompt_key, (), 0, N_DECODE)
    order = jax.vmap(shuffle_pages)(jax.random.split(order_key, N_DECODE)).astype(jnp.int32)
    spare = jax.vmap(shuffle_slots)(jax.random.split(slot_key, N_DECODE)).astype(jnp.int32)
    every = jax.vmap(shuffle_every)(jax.random.split(every_key, N_DECODE)).astype(jnp.int32)
    first = jnp.full((N_DECODE, CAP), busy, jnp.int32)
    others = (busy + 1 + spare[:, :PAGES - CAP] // CAP) % N_DECODE
    pinned = jnp.concatenate([first, others.astype(jnp.int32)], axis=1)
    spread = (every[:, :PAGES] // CAP).astype(jnp.int32)
    rows = jnp.arange(N_DECODE, dtype=jnp.int32)[:, None]
    by_position = jnp.where(rows == chosen, pinned, spread)
    return jax.vmap(place_owners)(order, by_position).astype(jnp.int32)


def steps_of(own_key, dims, pieces, least, high):
    level, own = 1.0, jax.random.fold_in(own_key, 6)
    for position, parts in pieces:
        draws = jnp.exp(jax.random.uniform(jax.random.fold_in(own, position), (parts,), jnp.float32, least / len(pieces), high / len(pieces)))
        level = level * jnp.repeat(draws, dims[position] // parts).reshape([-1 if axis == position else 1 for axis in range(len(dims))])
    return level


def centred(stream_key, shape, deviation, most, pieces=(), held_as=jnp.bfloat16):
    loudness = steps_of(stream_key, shape, pieces, -0.22, 0.18) if pieces else 1.0
    array = jax.random.normal(stream_key, shape, jnp.float32) * deviation * loudness
    return jnp.minimum(jnp.maximum(array, -most), most).astype(held_as)


def setup_inputs(seed: int = 0) -> dict:
    seeds = jax.random.split(jax.random.key(seed), 11)
    hidden_in = draw_hidden_in(jax.random.fold_in(seeds[10], 71), 0)
    norm_gain = jnp.clip(jnp.exp(jax.random.uniform(seeds[1], (D,), jnp.float32, math.log(0.5), math.log(2.0))), 0.5, 2.0)
    w_query = centred(seeds[2], (D, HEADS * HD), D ** -0.5, 0.0625, ((0, 16), (1, 8)))
    w_key = centred(seeds[3], (D, KV_HEADS * HD), D ** -0.5, 0.0625, ((0, 16), (1, 8)))
    w_value = centred(seeds[4], (D, KV_HEADS * HD), D ** -0.5, 0.0625, ((0, 16), (1, 8)))
    w_out = centred(seeds[5], (HEADS * HD, D), 0.5, 3.0, ((0, 8), (1, 16)))
    cache_k = draw_cache_k(jax.random.fold_in(seeds[10], 71), 0)
    cache_v = centred(seeds[7], (N_DECODE, KV_HEADS, PREFIX, HD), 1.0, 6.0, ((0, 16), (1, 8)))
    prefix_len = draw_prefix_len(jax.random.fold_in(seeds[10], 71), 0)
    page_owner = draw_page_owner(jax.random.fold_in(seeds[10], 71), 0)
    return dict(hidden_in=hidden_in, norm_gain=norm_gain, w_query=w_query, w_key=w_key, w_value=w_value, w_out=w_out, cache_k=cache_k, cache_v=cache_v, prefix_len=prefix_len, page_owner=page_owner)


THETA = 500000.0
EPS = 1e-05

def rope_tables(positions, width):
    half = width // 2
    steps = jnp.arange(half, dtype=jnp.float32) * (2.0 / width)
    freqs = jnp.exp(-math.log(THETA) * steps)
    angles = positions.astype(jnp.float32)[:, None] * freqs[None, :]
    return (jnp.cos(angles), jnp.sin(angles))

def rotate(values, cosine, sine):
    half = values.shape[-1] // 2
    first = values[..., :half]
    second = values[..., half:]
    cos_part = cosine[:, None, :]
    sin_part = sine[:, None, :]
    return jnp.concatenate([first * cos_part - second * sin_part, second * cos_part + first * sin_part], axis=-1)

def attend_head(query, keys, values, allowed, factor):
    scores = jnp.dot(query, keys.T, preferred_element_type=jnp.float32) * factor
    scores = jnp.where(allowed, scores, -jnp.inf)
    top = lax.optimization_barrier(jnp.max(scores, axis=1, keepdims=True))
    expo = jnp.exp(scores - top)
    total = lax.optimization_barrier(jnp.sum(expo, axis=1, keepdims=True))
    weights = (expo / total).astype(jnp.bfloat16)
    return jnp.dot(weights, values, preferred_element_type=jnp.float32).astype(jnp.bfloat16)

def reference(hidden_in, norm_gain, w_query, w_key, w_value, w_out, cache_k, cache_v, prefix_len, page_owner):
    factor = 1.0 / math.sqrt(HD)

    def one_group(group):
        rows_in, keys_cached, values_cached, live = group
        rows = rows_in.astype(jnp.float32)
        mean_sq = lax.optimization_barrier(jnp.mean(rows * rows, axis=1, keepdims=True))
        normed = (rows * lax.rsqrt(mean_sq + EPS) * norm_gain).astype(jnp.bfloat16)
        q_raw = jnp.dot(normed, w_query, preferred_element_type=jnp.float32)
        k_raw = jnp.dot(normed, w_key, preferred_element_type=jnp.float32)
        v_raw = jnp.dot(normed, w_value, preferred_element_type=jnp.float32)
        positions = live + jnp.arange(SPAN, dtype=jnp.int32)
        cosine, sine = rope_tables(positions, HD)
        queries = rotate(q_raw.reshape(SPAN, HEADS, HD), cosine, sine).astype(jnp.bfloat16)
        keys = rotate(k_raw.reshape(SPAN, KV_HEADS, HD), cosine, sine).astype(jnp.bfloat16)
        values = v_raw.reshape(SPAN, KV_HEADS, HD).astype(jnp.bfloat16)
        column = jnp.arange(PREFIX + SPAN, dtype=jnp.int32)[None, :]
        row = jnp.arange(SPAN, dtype=jnp.int32)[:, None]
        allowed = jnp.where(column < PREFIX, column < live, column - PREFIX <= row)
        query_groups = jnp.transpose(queries.reshape(SPAN, KV_HEADS, QPK, HD), (1, 0, 2, 3))
        key_groups = jnp.transpose(keys, (1, 0, 2))
        value_groups = jnp.transpose(values, (1, 0, 2))

        def one_kv(pack):
            head_queries, new_keys, new_values, old_keys, old_values = pack
            all_keys = jnp.concatenate([old_keys, new_keys], axis=0)
            all_values = jnp.concatenate([old_values, new_values], axis=0)
            outs = [attend_head(head_queries[:, j, :], all_keys, all_values, allowed, factor) for j in range(QPK)]
            return jnp.concatenate(outs, axis=1)
        attended = lax.map(one_kv, (query_groups, key_groups, value_groups, keys_cached, values_cached))
        out_rows = w_out.reshape(KV_HEADS, QPK * HD, D).astype(jnp.float32)
        partial_terms = jnp.einsum('kcd,kde->kce', attended.astype(jnp.float32), out_rows).astype(jnp.bfloat16)
        partial_terms = lax.optimization_barrier(partial_terms)
        out_block = lax.optimization_barrier(jnp.sum(partial_terms.astype(jnp.float32), axis=0)).astype(jnp.bfloat16)
        both = jnp.stack([keys, values], axis=1).reshape(PAGES, PAGE, 2, KV_HEADS, HD)
        magnitude = lax.optimization_barrier(jnp.max(jnp.abs(both.astype(jnp.float32)), axis=(1, 4)))
        page_scale = (magnitude + 1e-06).astype(jnp.bfloat16)
        scaled = (both.astype(jnp.float32) / page_scale.astype(jnp.float32)[:, None, :, :, None]).astype(jnp.bfloat16)
        scaled = jnp.transpose(scaled, (0, 2, 1, 3, 4)).reshape(PAGES, 2, PAGE, KV_HEADS * HD)
        return (out_block, scaled, page_scale)
    attn_out, pages, scales = lax.map(one_group, (hidden_in, cache_k, cache_v, prefix_len))
    same = page_owner[:, :, None] == page_owner[:, None, :]
    earlier = jnp.arange(PAGES, dtype=jnp.int32)[None, None, :] < jnp.arange(PAGES, dtype=jnp.int32)[None, :, None]
    rank = lax.optimization_barrier(jnp.sum((same & earlier).astype(jnp.int32), axis=2))
    slot = jnp.arange(N_DECODE, dtype=jnp.int32)[:, None] * CAP + rank
    owned_pages = jnp.zeros((N_DECODE, N_DECODE * CAP, 2, PAGE, KV_HEADS * HD), jnp.bfloat16).at[page_owner, slot].set(pages)
    owned_scales = jnp.zeros((N_DECODE, N_DECODE * CAP, 2, KV_HEADS), jnp.bfloat16).at[page_owner, slot].set(scales)
    numbers = jnp.broadcast_to(jnp.arange(PAGES, dtype=jnp.int32)[None, :], (N_DECODE, PAGES))
    owned_ids = jnp.full((N_DECODE, N_DECODE * CAP), -1, jnp.int32).at[page_owner, slot].set(numbers)
    return (attn_out, owned_pages, owned_scales, owned_ids)
```

```python
import functools
import math

import jax
import jax.numpy as jnp
from jax import lax
from jax.experimental import pallas as pl
from jax.experimental.pallas import tpu as pltpu
from jax.sharding import PartitionSpec as P

CAP = 2
THETA = 500000.0
EPS = 1e-05
BF = jnp.bfloat16
F32 = jnp.float32
MB = 2**20


def tensor_perm(move):
    pairs = []
    for z in range(2):
        for x in range(4):
            a, b = move(z, x)
            pairs.append((z * 4 + x, a * 4 + b % 4))
    return pairs


def decode_perm(move):
    pairs = []
    for z in range(2):
        for y in range(4):
            for c in range(2):
                a, b, e = move(z, y, c)
                pairs.append((z * 8 + y * 2 + c, a * 8 + (b % 4) * 2 + e))
    return pairs


X_UP = tensor_perm(lambda z, x: (z, x + 1))
X_DOWN = tensor_perm(lambda z, x: (z, x - 1))
Z_SWAP = tensor_perm(lambda z, x: (1 - z, x))
Y_UP = decode_perm(lambda z, y, c: (z, y + 1, c))
Y_DOWN = decode_perm(lambda z, y, c: (z, y - 1, c))
ZH_SWAP = decode_perm(lambda z, y, c: (1 - z, y, c))
CORE_SWAP = decode_perm(lambda z, y, c: (z, y, 1 - c))
X_GROUPS = [[0, 1, 2, 3], [4, 5, 6, 7]]


def to_t(value, pairs):
    return lax.ppermute(value, "tensor", pairs)


def to_d(value, pairs):
    return lax.ppermute(value, "decode", pairs)


def gather_rows(own, z, x):
    h = own.shape[0] // 2
    left = to_t(own, X_UP)
    right = to_t(own, X_DOWN)
    over = to_t(own, Z_SWAP)
    over_left_a = to_t(left[:h], Z_SWAP)
    over_right_b = to_t(right[h:], Z_SWAP)
    over_left_b = to_t(over[h:], X_UP)
    over_right_a = to_t(over[:h], X_DOWN)
    far_a = to_t(left[:h], X_UP)
    far_b = to_t(right[h:], X_DOWN)
    over_far_b = to_t(over_left_b, X_UP)
    over_far_a = to_t(over_right_a, X_DOWN)
    here, there = z * 4, (1 - z) * 4
    lo, hi, far = (x + 3) % 4, (x + 1) % 4, (x + 2) % 4
    return [
        (own, here + x, 0),
        (left, here + lo, 0),
        (right, here + hi, 0),
        (over, there + x, 0),
        (over_left_a, there + lo, 0),
        (over_left_b, there + lo, h),
        (over_right_a, there + hi, 0),
        (over_right_b, there + hi, h),
        (far_a, here + far, 0),
        (far_b, here + far, h),
        (over_far_a, there + far, 0),
        (over_far_b, there + far, h),
    ]


def gather_shards(own, zh, y, core):
    h = own.shape[0] // 2
    over = to_d(own, ZH_SWAP)
    low = to_d(own, Y_UP)
    high = to_d(own, Y_DOWN)
    over_low = to_d(over, Y_UP)
    over_high = to_d(over, Y_DOWN)
    far_a = to_d(low[:h], Y_UP)
    far_b = to_d(high[h:], Y_DOWN)
    over_far_a = to_d(over_low[:h], Y_UP)
    over_far_b = to_d(over_high[h:], Y_DOWN)
    here, there = zh * 8 + core, (1 - zh) * 8 + core
    lo, hi, far = (y + 3) % 4 * 2, (y + 1) % 4 * 2, (y + 2) % 4 * 2
    whole = [
        (own, here + y * 2),
        (over, there + y * 2),
        (low, here + lo),
        (high, here + hi),
        (over_low, there + lo),
        (over_high, there + hi),
    ]
    halves = [
        (far_a, far_b, here + far),
        (over_far_a, over_far_b, there + far),
    ]
    flip = 1 - 2 * core
    whole = whole + [(to_d(a, CORE_SWAP), i + flip) for a, i in whole]
    halves = halves + [
        (to_d(a, CORE_SWAP), to_d(b, CORE_SWAP), i + flip) for a, b, i in halves
    ]
    return whole, halves


def hbm():
    return pl.BlockSpec(memory_space=pl.ANY)


def vmem():
    return pl.BlockSpec(memory_space=pltpu.VMEM)


def smem():
    return pl.BlockSpec(memory_space=pltpu.SMEM)


def load_shards(refs, place, sems):
    for i in range(12):
        pltpu.make_async_copy(refs[i], place(i, None), sems.at[i]).start()
    for i in range(4):
        for half in range(2):
            ref = refs[12 + 2 * i + half]
            pltpu.make_async_copy(ref, place(12 + i, half), sems.at[12 + i]).start()


def flat_shards(whole, halves):
    arrays = [a for a, _ in whole] + [a for p in halves for a in p[:2]]
    index = jnp.stack([i for _, i in whole] + [p[2] for p in halves]).astype(jnp.int32)
    return arrays, index


def project_kernel(n_rows, rot_scale, x_at, w_at, cos_ref, sin_ref, *refs):
    xs, ws = refs[:n_rows], refs[n_rows : n_rows + 20]
    q_ref, k_ref, v_ref, xv, wv, acc, xsem, wsem = refs[n_rows + 20 :]
    copies = []
    for i, ref in enumerate(xs):
        for part in range(ref.shape[0] // 32):
            to = pl.multiple_of(x_at[2 * i + part], 32)
            copies.append(
                pltpu.make_async_copy(
                    ref.at[pl.ds(part * 32, 32), :],
                    xv.at[pl.ds(to, 32), :],
                    xsem.at[2 * i + part],
                )
            )
    for copy in copies:
        copy.start()
    depth = ws[0].shape[0]

    def place(i, half):
        base = pl.multiple_of(w_at[i] * depth, depth)
        if half is None:
            return wv.at[pl.ds(base, depth), :]
        return wv.at[pl.ds(base + half * (depth // 2), depth // 2), :]

    load_shards(ws, place, wsem)
    for copy in copies:
        copy.wait()

    def step(i, carry):
        base = pl.multiple_of(w_at[i] * depth, depth)
        part = wv.at[pl.ds(base, depth), :]
        pltpu.make_async_copy(part, part, wsem.at[i]).wait()
        term = jnp.dot(xv[:, pl.ds(base, depth)], part[...], preferred_element_type=F32)

        @pl.when(i == 0)
        def _():
            acc[...] = term

        @pl.when(i > 0)
        def _():
            acc[...] += term

        return carry

    lax.fori_loop(0, 16, step, 0)
    cos, sin = cos_ref[...], sin_ref[...]
    heads = q_ref.shape[0]

    def rotated(j):
        part = acc[:, j * 128 : (j + 1) * 128]
        return part * cos + pltpu.roll(part, 64, 1) * sin

    for j in range(heads):
        q_ref[j] = (rotated(j) * rot_scale).astype(BF)
    keys = rotated(heads).astype(BF)
    values = acc[:, (heads + 1) * 128 :].astype(BF)
    half = keys.shape[0] // 2
    for s in range(half // 32):
        for r in range(2):
            rows = slice(r * half + s * 32, r * half + s * 32 + 32)
            to = slice(s * 64 + r * 32, s * 64 + r * 32 + 32)
            k_ref[to, :] = keys[rows]
            v_ref[to, :] = values[rows]


def project(pieces, whole, halves, cosine, sine, span):
    arrays = [a for a, _, _ in pieces]
    width = arrays[0].shape[1]
    at = []
    for a, source, offset in pieces:
        for part in range(2):
            first = offset + part * 32
            at.append(source * 32 + (first // 32 % 2) * (span // 2))
    ws, index = flat_shards(whole, halves)
    cols = ws[0].shape[1]
    heads = cols // 128 - 2
    scale = math.log2(math.e) / math.sqrt(128)
    n = len(arrays)
    return pl.pallas_call(
        functools.partial(project_kernel, n, scale),
        in_specs=[smem(), smem(), vmem(), vmem()] + [hbm()] * (n + 20),
        out_specs=[vmem()] * 3,
        out_shape=[
            jax.ShapeDtypeStruct((heads, span, 128), BF),
            jax.ShapeDtypeStruct((span, 128), BF),
            jax.ShapeDtypeStruct((span, 128), BF),
        ],
        scratch_shapes=[
            pltpu.VMEM((span, width), BF),
            pltpu.VMEM((width, cols), BF),
            pltpu.VMEM((span, cols), F32),
            pltpu.SemaphoreType.DMA((2 * n,)),
            pltpu.SemaphoreType.DMA((16,)),
        ],
        compiler_params=pltpu.CompilerParams(vmem_limit_bytes=40 * MB),
        cost_estimate=pl.CostEstimate(
            flops=2 * span * width * cols, bytes_accessed=24 * MB, transcendentals=0
        ),
        name="project",
    )(jnp.stack(at).astype(jnp.int32), index, cosine, sine, *arrays, *ws)


def attend_kernel(chunk, block, live_ref, q_ref, k_ref, v_ref, kn_ref, vn_ref, o_ref):
    live = live_ref[0]
    q = q_ref[0]

    def update(state, keys, values, allowed):
        s = lax.dot_general(q, keys, (((1,), (1,)), ((), ())), preferred_element_type=F32)
        if allowed is not None:
            s = jnp.where(allowed(s.shape), s, -1e30)
        top = jnp.max(s, axis=1, keepdims=True)
        if state is not None:
            top = jnp.maximum(state[0], top)
        p = jnp.exp2(s - top)
        total = sum(p[:, c * 128 : (c + 1) * 128] for c in range(p.shape[1] // 128))
        out = jnp.dot(p.astype(BF), values, preferred_element_type=F32)
        if state is None:
            return top, total, out
        keep = jnp.exp2(state[0] - top)
        return top, state[1] * keep + total, state[2] * keep + out

    def cached(j, state, allowed=None):
        at = pl.ds(pl.multiple_of(j * block, block), block)
        return update(state, k_ref[at, :], v_ref[at, :], allowed)

    def new_allowed(shape):
        i = lax.broadcasted_iota(jnp.int32, shape, 0)
        row = i // 32 * 64 + chunk * 32 + i % 32
        return lax.broadcasted_iota(jnp.int32, shape, 1) <= row

    full = live // block
    state = update(None, kn_ref[...], vn_ref[...], new_allowed)
    state = lax.fori_loop(0, full, cached, state)
    left = live - full * block

    def last(state):
        return cached(
            full, state, lambda shape: lax.broadcasted_iota(jnp.int32, shape, 1) < left
        )

    top, total, out = lax.cond(left > 0, last, lambda s: s, state)
    o_ref[...] = (out / jnp.sum(total, axis=1, keepdims=True)).astype(BF)


def attend(chunk, q, cache_k, cache_v, keys, values, live):
    heads, span, width = q.shape
    rows = span // 2
    prefix = cache_k.shape[0]
    block = 2048
    return pl.pallas_call(
        functools.partial(attend_kernel, chunk, block),
        grid=(heads,),
        in_specs=[
            smem(),
            pl.BlockSpec((1, rows, width), lambda i: (i, chunk, 0)),
            vmem(),
            vmem(),
            vmem(),
            vmem(),
        ],
        out_specs=pl.BlockSpec((rows, width), lambda i: (0, i)),
        out_shape=jax.ShapeDtypeStruct((rows, heads * width), BF),
        compiler_params=pltpu.CompilerParams(vmem_limit_bytes=40 * MB),
        cost_estimate=pl.CostEstimate(
            flops=4 * heads * rows * (prefix + span) * width,
            bytes_accessed=4 * prefix * width,
            transcendentals=heads * rows * (prefix + span),
        ),
        name="attend",
    )(live, q, cache_k, cache_v, keys, values)


def output_kernel(x_at, w_at, z_at, a0, a1, a2, a3, a4, *refs):
    ws = refs[:20]
    send_ref, keep_ref, xv, wv, xsem, wsem = refs[20:]
    width = a0.shape[1]
    half = a3.shape[0]
    copies = []
    for i, (ref, row) in enumerate(((a0, 0), (a1, 0), (a2, 0), (a3, 0), (a4, half))):
        to = pl.multiple_of(x_at[i] * width, width)
        copies.append(
            pltpu.make_async_copy(
                ref, xv.at[pl.ds(row, ref.shape[0]), pl.ds(to, width)], xsem.at[i]
            )
        )
    for copy in copies:
        copy.start()
    depth, cols = ws[0].shape

    def place(i, part):
        to = pl.multiple_of(w_at[i] * cols, cols)
        if part is None:
            return wv.at[:, pl.ds(to, cols)]
        return wv.at[pl.ds(part * (depth // 2), depth // 2), pl.ds(to, cols)]

    load_shards(ws, place, wsem)
    for copy in copies:
        copy.wait()
    for i in range(16):
        part = place(i, None)
        pltpu.make_async_copy(part, part, wsem.at[i]).wait()
    theirs = pl.multiple_of((1 - z_at[0]) * half, half)
    mine = pl.multiple_of(z_at[0] * half, half)

    def step(i, carry):
        at = pl.ds(pl.multiple_of(i * 512, 512), 512)
        w = wv[:, at]
        send_ref[:, at] = jnp.dot(
            xv[pl.ds(theirs, half), :], w, preferred_element_type=F32
        ).astype(BF)
        keep_ref[:, at] = jnp.dot(xv[pl.ds(mine, half), :], w, preferred_element_type=F32)
        return carry

    lax.fori_loop(0, wv.shape[1] // 512, step, 0)


def output(attended, whole, halves, z, x):
    half = attended.shape[0] // 2
    left = to_t(attended, X_UP)
    right = to_t(attended, X_DOWN)
    far_a = to_t(left[:half], X_UP)
    far_b = to_t(right[half:], X_DOWN)
    far = (x + 2) % 4
    at = jnp.stack([x, (x + 3) % 4, (x + 1) % 4, far, far]).astype(jnp.int32)
    ws, index = flat_shards(whole, halves)
    depth, cols = ws[0].shape
    return pl.pallas_call(
        output_kernel,
        in_specs=[smem()] * 3 + [hbm()] * 25,
        out_specs=[vmem()] * 2,
        out_shape=[
            jax.ShapeDtypeStruct((half, 16 * cols), BF),
            jax.ShapeDtypeStruct((half, 16 * cols), F32),
        ],
        scratch_shapes=[
            pltpu.VMEM((2 * half, depth), BF),
            pltpu.VMEM((depth, 16 * cols), BF),
            pltpu.SemaphoreType.DMA((5,)),
            pltpu.SemaphoreType.DMA((16,)),
        ],
        compiler_params=pltpu.CompilerParams(vmem_limit_bytes=40 * MB),
        cost_estimate=pl.CostEstimate(
            flops=4 * half * depth * 16 * cols, bytes_accessed=11 * MB, transcendentals=0
        ),
        name="output",
    )(at, index, z[None].astype(jnp.int32), attended, left, right, far_a, far_b, *ws)


def place_kernel(pages, w_at, page_of, *refs):
    ws = refs[:20]
    out_ref, scale_ref, wv, wsem = refs[20:]
    depth, cols = ws[0].shape
    page = depth // pages

    def place(i, part):
        base = pl.multiple_of(w_at[i] * depth, depth)
        if part is None:
            return wv.at[pl.ds(base, depth), :]
        return wv.at[pl.ds(base + part * (depth // 2), depth // 2), :]

    load_shards(ws, place, wsem)
    for i in range(16):
        part = place(i, None)
        pltpu.make_async_copy(part, part, wsem.at[i]).wait()

    def slot(s, carry):
        number = page_of[s]

        @pl.when(number < 0)
        def _():
            out_ref[s] = jnp.zeros(out_ref.shape[1:], BF)
            scale_ref[s] = jnp.zeros(scale_ref.shape[1:], F32)

        @pl.when(number >= 0)
        def _():
            at = pl.multiple_of(s // CAP * depth + number * page, page)
            rows = wv[pl.ds(at, page), :].astype(F32)
            for c in range(2):
                part = rows[:, c * 128 : (c + 1) * 128]
                most = jnp.max(jnp.max(jnp.abs(part), axis=0, keepdims=True), axis=1, keepdims=True)
                scale = (most + 1e-06).astype(BF).astype(F32)
                out_ref[s, c] = (part / scale).astype(BF)
                scale_ref[s, c : c + 1, :] = jnp.broadcast_to(scale, (1, 128))

        return carry

    lax.fori_loop(0, out_ref.shape[0], slot, 0)


def place_pages(keys, values, owners, zh, y, core, d):
    groups, count = owners.shape
    span = keys.shape[0]
    order = jnp.arange(count, dtype=jnp.int32)
    same = owners[:, :, None] == owners[:, None, :]
    rank = jnp.sum((same & (order[None, :] < order[:, None])[None]).astype(jnp.int32), axis=2)
    mine = (owners == d)[:, None, :] & (rank[:, None, :] == jnp.arange(CAP)[None, :, None])
    ids = jnp.max(jnp.where(mine, order[None, None, :], -1), axis=2).reshape(groups * CAP)
    whole, halves = gather_shards(jnp.concatenate([keys, values], axis=1), zh, y, core)
    ws, index = flat_shards(whole, halves)
    pages, scales = pl.pallas_call(
        functools.partial(place_kernel, count),
        in_specs=[smem()] * 2 + [hbm()] * 20,
        out_specs=[vmem()] * 2,
        out_shape=[
            jax.ShapeDtypeStruct((groups * CAP, 2, span // count, 128), BF),
            jax.ShapeDtypeStruct((groups * CAP, 2, 128), F32),
        ],
        scratch_shapes=[
            pltpu.VMEM((groups * span, 256), BF),
            pltpu.SemaphoreType.DMA((16,)),
        ],
        compiler_params=pltpu.CompilerParams(vmem_limit_bytes=24 * MB),
        cost_estimate=pl.CostEstimate(
            flops=4 * MB, bytes_accessed=8 * MB, transcendentals=0
        ),
        name="place",
    )(index, ids, *ws)
    return pages[None], scales[None, :, :, :1].astype(BF), ids[None]


def rope_tables(positions, width):
    half = width // 2
    steps = jnp.arange(half, dtype=F32) * (2.0 / width)
    freqs = jnp.exp(-math.log(THETA) * steps)
    angles = positions.astype(F32)[:, None] * freqs[None, :]
    cosine, sine = jnp.cos(angles), jnp.sin(angles)
    return (
        jnp.concatenate([cosine, cosine], axis=1),
        jnp.concatenate([-sine, sine], axis=1),
    )


def body(
    hidden_in, norm_gain, w_query, w_key, w_value, w_out, cache_k, cache_v, prefix_len, page_owner
):
    t, d = lax.axis_index("tensor"), lax.axis_index("decode")
    z, x = t // 4, t % 4
    zh, y, core = d // 8, d // 2 % 4, d % 2
    span = hidden_in.shape[1] * 8
    width = cache_k.shape[-1]
    owners = lax.all_gather(page_owner, "decode", axis=0, tiled=True)
    rows = hidden_in[0].astype(F32)
    mean_sq = jnp.mean(rows * rows, axis=1, keepdims=True)
    normed = (rows * lax.rsqrt(mean_sq + EPS) * norm_gain).astype(BF)
    weights = gather_shards(
        jnp.concatenate([w_query, w_key, w_value], axis=1), zh, y, core
    )
    pieces = gather_rows(normed, z, x)
    i = jnp.arange(span, dtype=jnp.int32)
    true_row = i % (span // 2) // 32 * 64 + i // (span // 2) * 32 + i % 32
    cosine, sine = rope_tables(prefix_len[0] + true_row, width)
    queries, keys, values = project(pieces, *weights, cosine, sine, span)
    depth, cols = w_out.shape
    quarters = w_out.reshape(depth, 4, cols // 4).transpose(1, 0, 2)
    quarters = lax.all_to_all(
        quarters, "tensor", 0, 0, axis_index_groups=X_GROUPS, tiled=True
    )
    out_weights = gather_shards(quarters.reshape(4 * depth, cols // 4), zh, y, core)
    parts = []
    for chunk in range(2):
        attended = attend(chunk, queries, cache_k[0, 0], cache_v[0, 0], keys, values, prefix_len)
        send, keep = output(attended, *out_weights, z, x)
        summed = (keep + to_t(send, Z_SWAP).astype(F32)).astype(BF)
        back = lax.all_to_all(
            summed, "tensor", 0, 0, axis_index_groups=X_GROUPS, tiled=True
        )
        back = back.reshape(4, 32, 16, cols // 4).transpose(1, 2, 0, 3)
        parts.append(back.reshape(32, 16 * cols))
    attn_out = jnp.concatenate(parts, axis=0)[None]
    placed = place_pages(keys, values, owners, zh, y, core, d)
    return (attn_out, *placed)


def solution(mesh):
    in_specs = (
        P("decode", "tensor", None),
        P(),
        P("decode", "tensor"),
        P("decode", "tensor"),
        P("decode", "tensor"),
        P("tensor", "decode"),
        P("decode", "tensor", None, None),
        P("decode", "tensor", None, None),
        P("decode"),
        P("decode", None),
    )
    out_specs = (
        P("decode", "tensor", None),
        P("decode", None, None, None, "tensor"),
        P("decode", None, None, "tensor"),
        P("decode", None),
    )
    return jax.shard_map(body, mesh=mesh, in_specs=in_specs, out_specs=out_specs, check_vma=False)
```

```python
import functools
import math

import jax
import jax.numpy as jnp
from jax import lax
from jax.experimental import pallas as pl
from jax.experimental.pallas import tpu as pltpu
from jax.sharding import PartitionSpec as P

CAP = 2
THETA = 500000.0
EPS = 1e-05
BF = jnp.bfloat16
F32 = jnp.float32
MB = 2**20


def tensor_perm(move):
    pairs = []
    for z in range(2):
        for x in range(4):
            a, b = move(z, x)
            pairs.append((z * 4 + x, a * 4 + b % 4))
    return pairs


def decode_perm(move):
    pairs = []
    for z in range(2):
        for y in range(4):
            for c in range(2):
                a, b, e = move(z, y, c)
                pairs.append((z * 8 + y * 2 + c, a * 8 + (b % 4) * 2 + e))
    return pairs


X_UP = tensor_perm(lambda z, x: (z, x + 1))
X_DOWN = tensor_perm(lambda z, x: (z, x - 1))
Z_SWAP = tensor_perm(lambda z, x: (1 - z, x))
Y_UP = decode_perm(lambda z, y, c: (z, y + 1, c))
Y_DOWN = decode_perm(lambda z, y, c: (z, y - 1, c))
ZH_SWAP = decode_perm(lambda z, y, c: (1 - z, y, c))
CORE_SWAP = decode_perm(lambda z, y, c: (z, y, 1 - c))
X_FAR = tensor_perm(lambda z, x: (z, x + 2))


def to_t(value, pairs):
    return lax.ppermute(value, "tensor", pairs)


def to_d(value, pairs):
    return lax.ppermute(value, "decode", pairs)


def after(value, *others):
    return lax.optimization_barrier((value, *others))[0]


def together(*values):
    return lax.optimization_barrier(values)


def gather_inputs(rows, w, out, tables):
    h = w.shape[0] // 2
    low, high = to_d(w, Y_UP), to_d(w, Y_DOWN)
    left, right, over = to_t(rows, X_UP), to_t(rows, X_DOWN), to_t(rows, Z_SWAP)
    low, high, left, right, over = together(low, high, left, right, over)
    w_over = to_d(after(w, low), ZH_SWAP)
    far_low = to_d(low, Y_UP)
    far = to_t(left, X_UP)
    over_right = to_t(over, X_DOWN)
    far, over_right, w_over, far_low, out, *tables = together(
        far, over_right, w_over, far_low, out, *tables
    )
    over_left = to_t(after(over, far), X_UP)
    over_far = to_t(over_right, X_DOWN)
    over_low, over_high = to_d(w_over, Y_UP), to_d(w_over, Y_DOWN)
    over_left, over_far, over_low, over_high = together(over_left, over_far, over_low, over_high)
    far_a, far_b = to_d(over_low[:h], Y_UP), to_d(over_high[h:], Y_DOWN)
    return (
        [rows, left, right, far, over, over_left, over_right, over_far],
        [w, low, high, far_low, w_over, over_low, over_high],
        [far_a, far_b],
        tables,
        out,
    )


def row_sources(z, x):
    here, there = z * 4, (1 - z) * 4
    lo, hi, end = (x + 3) % 4, (x + 1) % 4, (x + 2) % 4
    return jnp.stack([first + at for first in (here, there) for at in (x, lo, hi, end)])


def shard_sources(zh, y):
    here, there = zh * 4, (1 - zh) * 4
    lo, hi, end = (y + 3) % 4, (y + 1) % 4, (y + 2) % 4
    return jnp.stack([first + at for first in (here, there) for at in (y, lo, hi, end)])


def stack_out(pieces, x):
    depth, wide = pieces[0].shape

    def kernel(x_ref, a0, a1, a2, a3, o_ref):
        for i, ref in enumerate((a0, a1, a2, a3)):
            to = pl.multiple_of((x_ref[0] + i) % 4 * depth, depth)
            o_ref[pl.ds(to, depth), :] = ref[...]

    return pl.pallas_call(
        kernel,
        in_specs=[smem()] + [vmem()] * 4,
        out_specs=vmem(),
        out_shape=jax.ShapeDtypeStruct((4 * depth, wide), BF),
        name="stack",
    )(x[None].astype(jnp.int32), *pieces)


def hbm():
    return pl.BlockSpec(memory_space=pltpu.HBM)


def vmem():
    return pl.BlockSpec(memory_space=pltpu.VMEM)


def smem():
    return pl.BlockSpec(memory_space=pltpu.SMEM)


def prepare_kernel(at_ref, h_ref, gain_ref, wq, wk, wv, wo, keep_ref, send_ref, w_ref, *parts):
    q_cols, k_cols = wq.shape[1], wk.shape[1]
    w_ref[:, :q_cols] = wq[...]
    w_ref[:, q_cols : q_cols + k_cols] = wk[...]
    w_ref[:, q_cols + k_cols :] = wv[...]
    rows, width = h_ref.shape
    depth = wq.shape[0]
    even_core = at_ref[0] == 0
    wide = wo.shape[1] // 4
    for j, part in enumerate(parts):
        to = pl.multiple_of((at_ref[1] + j) % 4 * wide, wide)
        part[...] = wo[:, pl.ds(to, wide)]

    def step(i, carry):
        at = pl.ds(pl.multiple_of(i * 16, 16), 16)
        h = h_ref[at, :].astype(F32)
        mean_sq = jnp.sum(h * h, axis=1, keepdims=True) / width
        normed = (h * lax.rsqrt(mean_sq + EPS) * gain_ref[...]).astype(BF)
        for k in range(width // (2 * depth)):
            even = normed[:, 2 * k * depth : (2 * k + 1) * depth]
            odd = normed[:, (2 * k + 1) * depth : (2 * k + 2) * depth]
            keep_ref[at, k * depth : (k + 1) * depth] = jnp.where(even_core, even, odd)
            send_ref[at, k * depth : (k + 1) * depth] = jnp.where(even_core, odd, even)
        return carry

    lax.fori_loop(0, rows // 16, step, 0)


def prepare(hidden, gain, w_query, w_key, w_value, w_out, core, x):
    rows, width = hidden.shape
    depth = w_query.shape[0]
    cols = w_query.shape[1] + 2 * w_key.shape[1]
    return pl.pallas_call(
        prepare_kernel,
        in_specs=[smem()] + [vmem()] * 6,
        out_specs=[vmem()] * 7,
        out_shape=[
            jax.ShapeDtypeStruct((rows, width // 2), BF),
            jax.ShapeDtypeStruct((rows, width // 2), BF),
            jax.ShapeDtypeStruct((depth, cols), BF),
        ]
        + [jax.ShapeDtypeStruct((w_out.shape[0], w_out.shape[1] // 4), BF)] * 4,
        compiler_params=pltpu.CompilerParams(vmem_limit_bytes=60 * MB),
        name="prepare",
    )(jnp.stack([core, x]).astype(jnp.int32), hidden, gain[None], w_query, w_key, w_value, w_out)


def project_kernel(x_at, w_at, *refs):
    xs, ws = refs[:8], refs[8:15]
    keep_ref, send_ref, xv, wv, xsem, wsem = refs[15:]
    span, cols = keep_ref.shape
    depth = ws[0].shape[0]
    half = xv.shape[1] // 2
    columns = []
    for g in range(2):
        columns.append(pl.ds(pl.multiple_of(w_at[4 * g] // 4 * half, half), half))
        for i, ref in enumerate(xs):
            for part in range(4):
                to = pl.multiple_of(x_at[i] * 32 + part * (span // 2), 32)
                pltpu.make_async_copy(
                    ref.at[pl.ds(part * 32, 32), columns[g]],
                    xv.at[pl.ds(to, 32), columns[g]],
                    xsem.at[g],
                ).start()
        for i in range(4 * g, min(4 * g + 4, 7)):
            to = pl.multiple_of(w_at[i] * depth, depth)
            pltpu.make_async_copy(ws[i], wv.at[pl.ds(to, depth), :], wsem.at[g]).start()
    missing = pl.multiple_of(w_at[7] * depth, depth)
    wv[pl.ds(missing, depth), :] = jnp.zeros((depth, cols), BF)
    for g in range(2):
        arrived = xv.at[:, columns[g]]
        pltpu.make_async_copy(arrived, arrived, xsem.at[g]).wait()
        arrived = wv.at[pl.ds(0, (4 - g) * depth), :]
        pltpu.make_async_copy(arrived, arrived, wsem.at[g]).wait()

        def step(i, carry, g=g):
            at = pl.ds(pl.multiple_of(i * 256, 256), 256)
            for p, ref in enumerate((keep_ref, send_ref)):
                term = jnp.dot(
                    xv[p * span : (p + 1) * span, columns[g]],
                    wv[columns[g], at],
                    preferred_element_type=F32,
                )
                ref[:, at] = term if g == 0 else ref[:, at] + term
            return carry

        lax.fori_loop(0, cols // 256, step, 0)


def project(rows, x_at, shards, w_at):
    span, width = rows[0].shape[0] * 4, rows[0].shape[1]
    cols = shards[0].shape[1]
    return pl.pallas_call(
        project_kernel,
        in_specs=[smem()] * 2 + [hbm()] * 15,
        out_specs=[vmem()] * 2,
        out_shape=[jax.ShapeDtypeStruct((span, cols), F32)] * 2,
        scratch_shapes=[
            pltpu.VMEM((2 * span, width), BF),
            pltpu.VMEM((width, cols), BF),
            pltpu.SemaphoreType.DMA((2,)),
            pltpu.SemaphoreType.DMA((2,)),
        ],
        compiler_params=pltpu.CompilerParams(vmem_limit_bytes=60 * MB),
        cost_estimate=pl.CostEstimate(
            flops=4 * span * width * cols, bytes_accessed=18 * MB, transcendentals=0
        ),
        name="project",
    )(x_at, w_at, *rows, *shards)


def project_last_kernel(prompt, x_at, w_at, *refs):
    xs = refs[:8]
    wa_ref, wb_ref, before_ref, o_ref, xv, xsem = refs[8:]
    span = o_ref.shape[0]
    depth = 2 * wa_ref.shape[0]
    columns = pl.ds(pl.multiple_of(w_at[7] * depth, depth), depth)
    for i, ref in enumerate(xs):
        for part in range(2):
            to = pl.multiple_of(x_at[i] * 32 + part * (span // 2), 32)
            pltpu.make_async_copy(
                ref.at[pl.ds(prompt * 64 + part * 32, 32), columns],
                xv.at[pl.ds(to, 32), :],
                xsem,
            ).start()
    pltpu.make_async_copy(xv, xv, xsem).wait()
    a = jnp.dot(xv[:, : depth // 2], wa_ref[...], preferred_element_type=F32)
    b = jnp.dot(xv[:, depth // 2 :], wb_ref[...], preferred_element_type=F32)
    o_ref[...] = before_ref[...] + a + b


def project_last(prompt, rows, x_at, halves, w_at, before):
    span, cols = before.shape
    depth = 2 * halves[0].shape[0]
    return pl.pallas_call(
        functools.partial(project_last_kernel, prompt),
        in_specs=[smem()] * 2 + [hbm()] * 8 + [vmem()] * 3,
        out_specs=vmem(),
        out_shape=jax.ShapeDtypeStruct((span, cols), F32),
        scratch_shapes=[pltpu.VMEM((span, depth), BF), pltpu.SemaphoreType.DMA],
        compiler_params=pltpu.CompilerParams(vmem_limit_bytes=40 * MB),
        cost_estimate=pl.CostEstimate(
            flops=2 * span * depth * cols, bytes_accessed=5 * MB, transcendentals=0
        ),
        name="project_last",
    )(x_at, w_at, *rows, *halves, before)


def rotate_kernel(rot_scale, a_ref, b_ref, cos_ref, sin_ref, q_ref, k_ref, v_ref):
    cos, sin = cos_ref[...], sin_ref[...]
    heads = q_ref.shape[0]

    def total(j):
        at = slice(j * 128, (j + 1) * 128)
        return a_ref[:, at] + b_ref[:, at]

    def rotated(j):
        part = total(j)
        return part * cos + pltpu.roll(part, 64, 1) * sin

    for j in range(heads):
        q_ref[j] = (rotated(j) * rot_scale).astype(BF)
    keys = rotated(heads).astype(BF)
    values = total(heads + 1).astype(BF)
    half = keys.shape[0] // 2
    for s in range(half // 32):
        for r in range(2):
            rows = slice(r * half + s * 32, r * half + s * 32 + 32)
            to = slice(s * 64 + r * 32, s * 64 + r * 32 + 32)
            k_ref[to, :] = keys[rows]
            v_ref[to, :] = values[rows]


def rotate(own, got, cosine, sine):
    span, cols = own.shape
    heads = cols // 128 - 2
    scale = math.log2(math.e) / math.sqrt(128)
    return pl.pallas_call(
        functools.partial(rotate_kernel, scale),
        in_specs=[vmem()] * 4,
        out_specs=[vmem()] * 3,
        out_shape=[
            jax.ShapeDtypeStruct((heads, span, 128), BF),
            jax.ShapeDtypeStruct((span, 128), BF),
            jax.ShapeDtypeStruct((span, 128), BF),
        ],
        compiler_params=pltpu.CompilerParams(vmem_limit_bytes=60 * MB),
        name="rotate",
    )(own, got, cosine, sine)


def attend_kernel(chunk, block, live_ref, q_ref, k_hbm, v_hbm, kn_ref, vn_ref, o_ref, k_ref, v_ref, sems):
    live = live_ref[0]
    blocks = k_ref.shape[0] // block
    head = pl.program_id(0)

    def loads(j):
        at = pl.ds(pl.multiple_of(j * block, block), block)
        return (
            pltpu.make_async_copy(k_hbm.at[at, :], k_ref.at[at, :], sems.at[0, j]),
            pltpu.make_async_copy(v_hbm.at[at, :], v_ref.at[at, :], sems.at[1, j]),
        )

    @pl.when(head == 0)
    def _():
        for j in range(blocks):
            for load in loads(j):
                load.start()

    q = q_ref[0]
    full = live // block
    left = live - full * block

    def scores(keys, allowed):
        s = lax.dot_general(q, keys, (((1,), (1,)), ((), ())), preferred_element_type=F32)
        return s if allowed is None else jnp.where(allowed(s.shape), s, -1e30)

    def lanes(op, values):
        return functools.reduce(
            op, [values[:, c * 128 : (c + 1) * 128] for c in range(values.shape[1] // 128)]
        )

    def weigh(s, top, values):
        p = jnp.exp2(s - top)
        return lanes(jnp.add, p), jnp.dot(p.astype(BF), values, preferred_element_type=F32)

    def part(j):
        at = pl.ds(pl.multiple_of(j * block, block), block)
        return k_ref[at, :], v_ref[at, :]

    def arrive(j):
        @pl.when(head == 0)
        def _():
            for load in loads(j):
                load.wait()

    def part_allowed(shape):
        return lax.broadcasted_iota(jnp.int32, shape, 1) < left

    def new_allowed(shape):
        i = lax.broadcasted_iota(jnp.int32, shape, 0)
        row = i // 32 * 64 + chunk * 32 + i % 32
        return lax.broadcasted_iota(jnp.int32, shape, 1) <= row

    def every(one, state, await_block):
        def body(j, state):
            await_block(j)
            return one(state, *part(j), None)

        state = lax.fori_loop(1, full, body, state)

        def rest(j, carry):
            await_block(j)
            return carry

        lax.fori_loop(full, blocks, rest, 0)
        state = lax.cond(
            left > 0, lambda st: one(st, *part(full), part_allowed), lambda st: st, state
        )
        return one(state, kn_ref[...], vn_ref[...], new_allowed)

    def finish(total, out):
        o_ref[...] = (out / jnp.sum(total, axis=1, keepdims=True)).astype(BF)

    arrive(0)
    keys, values = part(0)
    s = scores(keys, None)
    first_top = jnp.max(s, axis=1, keepdims=True)
    first = weigh(s, first_top, values)

    def fixed(state, keys, values, allowed):
        most, total, out = state
        s = scores(keys, allowed)
        more, term = weigh(s, first_top, values)
        return jnp.maximum(most, lanes(jnp.maximum, s)), total + more, out + term

    start = jnp.broadcast_to(first_top, (q.shape[0], 128))
    most, total, out = every(fixed, (start, *first), arrive)
    finish(total, out)

    @pl.when(jnp.max(most - first_top) > 40.0)
    def _():
        def running(state, keys, values, allowed):
            top, total, out = state
            s = scores(keys, allowed)
            new_top = jnp.maximum(top, jnp.max(s, axis=1, keepdims=True))
            more, term = weigh(s, new_top, values)
            keep = jnp.exp2(top - new_top)
            return new_top, total * keep + more, out * keep + term

        _, total, out = every(running, (first_top, *first), lambda j: None)
        finish(total, out)


def attend(chunk, q, cache_k, cache_v, keys, values, live):
    heads, span, width = q.shape
    rows = span // 2
    prefix = cache_k.shape[0]
    block = 2048
    return pl.pallas_call(
        functools.partial(attend_kernel, chunk, block),
        grid=(heads,),
        in_specs=[
            smem(),
            pl.BlockSpec((1, rows, width), lambda i: (i, chunk, 0)),
            hbm(),
            hbm(),
            vmem(),
            vmem(),
        ],
        out_specs=pl.BlockSpec((rows, width), lambda i: (0, i)),
        out_shape=jax.ShapeDtypeStruct((rows, heads * width), BF),
        scratch_shapes=[
            pltpu.VMEM((prefix, width), BF),
            pltpu.VMEM((prefix, width), BF),
            pltpu.SemaphoreType.DMA((2, prefix // block)),
        ],
        compiler_params=pltpu.CompilerParams(vmem_limit_bytes=60 * MB),
        cost_estimate=pl.CostEstimate(
            flops=4 * heads * rows * (prefix + span) * width,
            bytes_accessed=4 * prefix * width,
            transcendentals=heads * rows * (prefix + span),
        ),
        name="attend",
    )(live, q, cache_k, cache_v, keys, values)


def output_kernel(x_at, a0, a1, a2, a3, w_ref, o_ref, xv, wv, xsem, wsem):
    shards, depth, cols = w_ref.shape
    width = a0.shape[1]
    copies = []
    for i, ref in enumerate((a0, a1, a2, a3)):
        to = pl.multiple_of(x_at[i] * width, width)
        copies.append(pltpu.make_async_copy(ref, xv.at[:, pl.ds(to, width)], xsem.at[i]))
    for copy in copies:
        copy.start()
    loads = []
    for i in range(shards // 4):
        group = pl.ds(4 * i, 4)
        loads.append(pltpu.make_async_copy(w_ref.at[group], wv.at[group], wsem.at[i]))
    for load in loads:
        load.start()
    for copy in copies:
        copy.wait()
    for i, load in enumerate(loads):
        load.wait()
        w = jnp.concatenate([wv[j] for j in range(4 * i, 4 * i + 4)], axis=1)
        o_ref[:, 4 * i * cols : 4 * (i + 1) * cols] = jnp.dot(
            xv[...], w, preferred_element_type=F32
        ).astype(BF)


def output(pieces, weights, x):
    rows, width = pieces[0].shape
    x_at = jnp.stack([x, (x + 3) % 4, (x + 1) % 4, (x + 2) % 4]).astype(jnp.int32)
    shards, depth, cols = weights.shape
    return pl.pallas_call(
        output_kernel,
        in_specs=[smem()] + [hbm()] * 5,
        out_specs=vmem(),
        out_shape=jax.ShapeDtypeStruct((rows, shards * cols), BF),
        scratch_shapes=[
            pltpu.VMEM((rows, 4 * width), BF),
            pltpu.VMEM((shards, depth, cols), BF),
            pltpu.SemaphoreType.DMA((4,)),
            pltpu.SemaphoreType.DMA((4,)),
        ],
        compiler_params=pltpu.CompilerParams(vmem_limit_bytes=60 * MB),
        cost_estimate=pl.CostEstimate(
            flops=2 * rows * depth * shards * cols, bytes_accessed=11 * MB, transcendentals=0
        ),
        name="output",
    )(x_at, *pieces, weights)


def finish_kernel(*refs):
    o_ref = refs[-1]
    for r, ref in enumerate(refs[:-1]):
        for x in range(4):
            total = ref[x].astype(F32) + ref[4 + x].astype(F32)
            total = total.astype(BF)
            for d in range(16):
                to = d * 512 + x * 128
                o_ref[r * 32 : r * 32 + 32, to : to + 128] = total[:, d * 128 : d * 128 + 128]


def finish(parts):
    rows = parts[0].shape[1] * len(parts)
    return pl.pallas_call(
        finish_kernel,
        in_specs=[vmem()] * len(parts),
        out_specs=vmem(),
        out_shape=jax.ShapeDtypeStruct((rows, parts[0].shape[2] * 4), BF),
        compiler_params=pltpu.CompilerParams(vmem_limit_bytes=60 * MB),
        name="finish",
    )(*parts)


def place_kernel(pages, page_of, kv_ref, out_ref, scale_ref):
    page = out_ref.shape[2]

    def slot(s, carry):
        number = page_of[s]

        @pl.when(number < 0)
        def _():
            out_ref[s] = jnp.zeros(out_ref.shape[1:], BF)
            scale_ref[s] = jnp.zeros(scale_ref.shape[1:], F32)

        @pl.when(number >= 0)
        def _():
            at = pl.multiple_of(number * page, page)
            rows = kv_ref[s // CAP, pl.ds(at, page), :].astype(F32)
            for c in range(2):
                part = rows[:, c * 128 : (c + 1) * 128]
                most = jnp.max(jnp.max(jnp.abs(part), axis=0, keepdims=True), axis=1, keepdims=True)
                scale = (most + 1e-06).astype(BF).astype(F32)
                out_ref[s, c] = (part / scale).astype(BF)
                scale_ref[s, c : c + 1, :] = jnp.broadcast_to(scale, (1, 128))

        return carry

    lax.fori_loop(0, out_ref.shape[0], slot, 0)


def gather_pages(keys, values, page_owner):
    count = page_owner.shape[1]
    span = keys.shape[0]
    owner_rows = jnp.pad(page_owner.astype(BF), ((0, 15), (0, 256 - count)))
    sent = jnp.concatenate([jnp.concatenate([keys, values], axis=1), owner_rows], axis=0)
    return lax.all_gather(sent, "decode", axis=0)


def place_pages(got, count, d):
    groups, span = got.shape[0], got.shape[1] - 16
    owners = got[:, span, :count].astype(jnp.int32)
    order = jnp.arange(count, dtype=jnp.int32)
    same = owners[:, :, None] == owners[:, None, :]
    rank = jnp.sum((same & (order[None, :] < order[:, None])[None]).astype(jnp.int32), axis=2)
    mine = (owners == d)[:, None, :] & (rank[:, None, :] == jnp.arange(CAP)[None, :, None])
    ids = jnp.max(jnp.where(mine, order[None, None, :], -1), axis=2).reshape(groups * CAP)
    pages, scales = pl.pallas_call(
        functools.partial(place_kernel, count),
        in_specs=[smem(), vmem()],
        out_specs=[vmem()] * 2,
        out_shape=[
            jax.ShapeDtypeStruct((groups * CAP, 2, span // count, 128), BF),
            jax.ShapeDtypeStruct((groups * CAP, 2, 128), F32),
        ],
        compiler_params=pltpu.CompilerParams(vmem_limit_bytes=60 * MB),
        cost_estimate=pl.CostEstimate(
            flops=4 * MB, bytes_accessed=8 * MB, transcendentals=0
        ),
        name="place",
    )(ids, got)
    return pages[None], scales[None, :, :, :1].astype(BF), ids[None]


def rope_tables(positions, width):
    half = width // 2
    steps = jnp.arange(half, dtype=F32) * (2.0 / width)
    freqs = jnp.exp(-math.log(THETA) * steps)
    angles = positions.astype(F32)[:, None] * freqs[None, :]
    cosine, sine = jnp.cos(angles), jnp.sin(angles)
    return (
        jnp.concatenate([cosine, cosine], axis=1),
        jnp.concatenate([-sine, sine], axis=1),
    )


def body(
    hidden_in, norm_gain, w_query, w_key, w_value, w_out, cache_k, cache_v, prefix_len, page_owner
):
    t, d = lax.axis_index("tensor"), lax.axis_index("decode")
    z, x = t // 4, t % 4
    zh, y, core = d // 8, d // 2 % 4, d % 2
    span = hidden_in.shape[1] * 8
    width = cache_k.shape[-1]
    i = jnp.arange(span, dtype=jnp.int32)
    true_row = i % (span // 2) // 32 * 64 + i // (span // 2) * 32 + i % 32
    tables = rope_tables(prefix_len[0] + true_row, width)
    keep, send, w, *quarters = prepare(
        hidden_in[0], norm_gain, w_query, w_key, w_value, w_out, core, x
    )
    moves = (X_UP, X_FAR, X_DOWN)
    quarters = [quarters[0]] + [to_t(a, pairs) for a, pairs in zip(quarters[1:], moves)]
    chip_rows = jnp.concatenate([keep, to_d(send, CORE_SWAP)], axis=0)
    chip_rows, *quarters = together(chip_rows, *quarters)
    out = stack_out([quarters[i] for i in (0, 3, 2, 1)], x)
    rows, shards, last, (cosine, sine), out = gather_inputs(chip_rows, w, out, tables)
    out_weights = lax.all_gather(out, "decode", axis=0)
    x_at = row_sources(z, x).astype(jnp.int32)
    w_at = shard_sources(zh, y).astype(jnp.int32)
    own, other = project(rows, x_at, shards, w_at)
    other = project_last(1, rows, x_at, last, w_at, other)
    own = project_last(0, rows, x_at, last, w_at, after(own, other))
    queries, keys, values = rotate(own, to_d(other, CORE_SWAP), cosine, sine)

    def attend_chunk(chunk, queries):
        return attend(chunk, queries, cache_k[0, 0], cache_v[0, 0], keys, values, prefix_len)

    def spread(attended):
        return [attended] + [to_t(attended, pairs) for pairs in (X_UP, X_DOWN, X_FAR)]

    def back(partial):
        got = lax.all_to_all(partial, "tensor", 0, 0, tiled=True)
        return got.reshape(8, 32, partial.shape[1])

    got = gather_pages(keys, values, page_owner)
    first = attend_chunk(0, queries)
    first_pieces = spread(first)
    second = attend_chunk(1, after(queries, first))
    first_pieces[0] = after(first_pieces[0], second)
    second_pieces = spread(second)
    first_partial = output(first_pieces, out_weights, x)
    first_partial, *second_pieces = together(first_partial, *second_pieces)
    first_back = back(first_partial)
    second_partial = output(second_pieces, out_weights, x)
    placed = place_pages(after(got, second_partial), page_owner.shape[1], d)
    first_back = after(first_back, second_partial)
    second_back = back(after(second_partial, first_back))
    second_back = after(second_back, placed[0])
    attn_out = finish([first_back, second_back])[None]
    return (attn_out, *placed)


def solution(mesh):
    in_specs = (
        P("decode", "tensor", None),
        P(),
        P("decode", "tensor"),
        P("decode", "tensor"),
        P("decode", "tensor"),
        P("tensor", "decode"),
        P("decode", "tensor", None, None),
        P("decode", "tensor", None, None),
        P("decode"),
        P("decode", None),
    )
    out_specs = (
        P("decode", "tensor", None),
        P("decode", None, None, None, "tensor"),
        P("decode", None, None, "tensor"),
        P("decode", None),
    )
    return jax.shard_map(body, mesh=mesh, in_specs=in_specs, out_specs=out_specs, check_vma=False)
```

```python
import functools
import math

import jax
import jax.numpy as jnp
from jax import lax
from jax.experimental import pallas as pl
from jax.experimental.pallas import tpu as pltpu
from jax.sharding import PartitionSpec as P

CAP = 2
THETA = 500000.0
EPS = 1e-05
BF = jnp.bfloat16
F32 = jnp.float32
MB = 2**20


def tensor_perm(move):
    pairs = []
    for z in range(2):
        for x in range(4):
            a, b = move(z, x)
            pairs.append((z * 4 + x, a * 4 + b % 4))
    return pairs


def decode_perm(move):
    pairs = []
    for z in range(2):
        for y in range(4):
            for c in range(2):
                a, b, e = move(z, y, c)
                pairs.append((z * 8 + y * 2 + c, a * 8 + (b % 4) * 2 + e))
    return pairs


X_UP = tensor_perm(lambda z, x: (z, x + 1))
X_DOWN = tensor_perm(lambda z, x: (z, x - 1))
Z_SWAP = tensor_perm(lambda z, x: (1 - z, x))
Y_UP = decode_perm(lambda z, y, c: (z, y + 1, c))
Y_DOWN = decode_perm(lambda z, y, c: (z, y - 1, c))
ZH_SWAP = decode_perm(lambda z, y, c: (1 - z, y, c))
CORE_SWAP = decode_perm(lambda z, y, c: (z, y, 1 - c))
PARITIES = [list(range(c, 16, 2)) for c in range(2)]
X_FAR = tensor_perm(lambda z, x: (z, x + 2))


def to_t(value, pairs):
    return lax.ppermute(value, "tensor", pairs)


def to_d(value, pairs):
    return lax.ppermute(value, "decode", pairs)


def after(value, *others):
    return lax.optimization_barrier((value, *others))[0]


def together(*values):
    return lax.optimization_barrier(values)


def gather_inputs(rows, w, w_at, out, tables):
    low, high = to_d(w, Y_UP), to_d(w, Y_DOWN)
    left, right, over = to_t(rows, X_UP), to_t(rows, X_DOWN), to_t(rows, Z_SWAP)
    low, high, left, right, over = together(low, high, left, right, over)
    w_over = to_d(after(w, low), ZH_SWAP)
    far_low = to_d(low, Y_UP)
    far = to_t(left, X_UP)
    over_right = to_t(over, X_DOWN)
    far, over_right, w_over, far_low, out, *tables = together(
        far, over_right, w_over, far_low, out, *tables
    )
    over_left = to_t(after(over, far), X_UP)
    over_far = to_t(over_right, X_DOWN)
    over_low, over_high = to_d(w_over, Y_UP), to_d(w_over, Y_DOWN)
    far_over = to_d(far_low, ZH_SWAP)
    early = [rows, left, right, far, over, over_right]
    here = [w, low, high, far_low]
    before = project_early(early, here, w_at)
    over_left, over_far, over_low, over_high, far_over, before, out = together(
        over_left, over_far, over_low, over_high, far_over, before, out
    )
    return (
        early + [over_left, over_far],
        here + [w_over, over_low, over_high, far_over],
        before,
        tables,
        out,
    )


def row_sources(z, x):
    here, there = z * 4, (1 - z) * 4
    lo, hi, end = (x + 3) % 4, (x + 1) % 4, (x + 2) % 4
    places = [here + at for at in (x, lo, hi, end)] + [there + at for at in (x, hi, lo, end)]
    return jnp.stack(places)


def shard_sources(zh, y):
    here, there = zh * 4, (1 - zh) * 4
    lo, hi, end = (y + 3) % 4, (y + 1) % 4, (y + 2) % 4
    return jnp.stack([first + at for first in (here, there) for at in (y, lo, hi, end)])


def stack_out(pieces, x):
    depth, wide = pieces[0].shape

    def kernel(x_ref, a0, a1, a2, a3, o_ref):
        for i, ref in enumerate((a0, a1, a2, a3)):
            to = pl.multiple_of((x_ref[0] + i) % 4 * depth, depth)
            for k in range(8):
                o_ref[k, pl.ds(to, depth), :] = ref[...]

    return pl.pallas_call(
        kernel,
        in_specs=[smem()] + [vmem()] * 4,
        out_specs=vmem(),
        out_shape=jax.ShapeDtypeStruct((8, 4 * depth, wide), BF),
        compiler_params=pltpu.CompilerParams(vmem_limit_bytes=60 * MB),
        name="stack",
    )(x[None].astype(jnp.int32), *pieces)


def hbm():
    return pl.BlockSpec(memory_space=pltpu.HBM)


def vmem():
    return pl.BlockSpec(memory_space=pltpu.VMEM)


def smem():
    return pl.BlockSpec(memory_space=pltpu.SMEM)


def prepare_kernel(at_ref, h_ref, gain_ref, wq, wk, wv, wo, keep_ref, send_ref, w_ref, *parts):
    q_cols, k_cols = wq.shape[1], wk.shape[1]
    w_ref[:, :q_cols] = wq[...]
    w_ref[:, q_cols : q_cols + k_cols] = wk[...]
    w_ref[:, q_cols + k_cols :] = wv[...]
    rows, width = h_ref.shape
    depth = wq.shape[0]
    even_core = at_ref[0] == 0
    wide = wo.shape[1] // 4
    for j, part in enumerate(parts):
        to = pl.multiple_of((at_ref[1] + j) % 4 * wide, wide)
        part[...] = wo[:, pl.ds(to, wide)]

    def step(i, carry):
        at = pl.ds(pl.multiple_of(i * 16, 16), 16)
        h = h_ref[at, :].astype(F32)
        mean_sq = jnp.sum(h * h, axis=1, keepdims=True) / width
        normed = (h * lax.rsqrt(mean_sq + EPS) * gain_ref[...]).astype(BF)
        for k in range(width // (2 * depth)):
            even = normed[:, 2 * k * depth : (2 * k + 1) * depth]
            odd = normed[:, (2 * k + 1) * depth : (2 * k + 2) * depth]
            keep_ref[at, k * depth : (k + 1) * depth] = jnp.where(even_core, even, odd)
            send_ref[at, k * depth : (k + 1) * depth] = jnp.where(even_core, odd, even)
        return carry

    lax.fori_loop(0, rows // 16, step, 0)


def prepare(hidden, gain, w_query, w_key, w_value, w_out, core, x):
    rows, width = hidden.shape
    depth = w_query.shape[0]
    cols = w_query.shape[1] + 2 * w_key.shape[1]
    return pl.pallas_call(
        prepare_kernel,
        in_specs=[smem()] + [vmem()] * 6,
        out_specs=[vmem()] * 7,
        out_shape=[
            jax.ShapeDtypeStruct((rows, width // 2), BF),
            jax.ShapeDtypeStruct((rows, width // 2), BF),
            jax.ShapeDtypeStruct((depth, cols), BF),
        ]
        + [jax.ShapeDtypeStruct((w_out.shape[0], w_out.shape[1] // 4), BF)] * 4,
        compiler_params=pltpu.CompilerParams(vmem_limit_bytes=60 * MB),
        name="prepare",
    )(jnp.stack([core, x]).astype(jnp.int32), hidden, gain[None], w_query, w_key, w_value, w_out)


def start_shards(refs, w_at, wv, sem):
    for i, ref in enumerate(refs):
        depth = ref.shape[0]
        to = pl.multiple_of(w_at[i] % 4 * depth, depth)
        pltpu.make_async_copy(ref, wv.at[pl.ds(to, depth), :], sem).start()


def project_early_kernel(w_at, *refs):
    xs, ws = refs[:6], refs[6:10]
    o_ref, xv, wv, xsem, wsem = refs[10:]
    rows, wide = xs[0].shape[0], xv.shape[1]
    columns = pl.ds(pl.multiple_of(w_at[0] // 4 * wide, wide), wide)
    for i, ref in enumerate(xs):
        to = xv.at[i * rows : (i + 1) * rows, :]
        pltpu.make_async_copy(ref.at[:, columns], to, xsem).start()
    start_shards(ws, w_at, wv, wsem)
    pltpu.make_async_copy(xv, xv, xsem).wait()
    pltpu.make_async_copy(wv, wv, wsem).wait()
    for n in range(o_ref.shape[1] // 256):
        at = slice(n * 256, n * 256 + 256)
        o_ref[:, at] = jnp.dot(xv[...], wv[:, at], preferred_element_type=F32)


def project_early(rows, shards, w_at):
    n = len(rows) * rows[0].shape[0]
    wide, cols = rows[0].shape[1] // 2, shards[0].shape[1]
    return pl.pallas_call(
        project_early_kernel,
        in_specs=[smem()] + [hbm()] * 10,
        out_specs=vmem(),
        out_shape=jax.ShapeDtypeStruct((n, cols), F32),
        scratch_shapes=[
            pltpu.VMEM((n, wide), BF),
            pltpu.VMEM((wide, cols), BF),
            pltpu.SemaphoreType.DMA,
            pltpu.SemaphoreType.DMA,
        ],
        compiler_params=pltpu.CompilerParams(vmem_limit_bytes=60 * MB),
        cost_estimate=pl.CostEstimate(flops=MB, bytes_accessed=MB, transcendentals=0),
        name="project_early",
    )(w_at, *rows, *shards)


def project_kernel(prompt, x_at, w_at, *refs):
    xs, ws, before = refs[:8], refs[8:16], refs[16]
    o_ref, there, here, bv, wt, wh, acc, sems = refs[17:]
    wide = there.shape[1]
    part = o_ref.shape[0] // 8
    mine = pl.ds(prompt * part, part)
    side = w_at[0] // 4
    here_columns = pl.ds(pl.multiple_of(side * wide, wide), wide)
    there_columns = pl.ds(pl.multiple_of((1 - side) * wide, wide), wide)
    for i, ref in enumerate(xs):
        to = there.at[i * part : (i + 1) * part, :]
        pltpu.make_async_copy(ref.at[mine, there_columns], to, sems.at[0]).start()
    for i, ref in enumerate(ws[4:]):
        depth = ref.shape[0]
        to = pl.multiple_of(w_at[4 + i] % 4 * depth, depth)
        pltpu.make_async_copy(ref, wt.at[pl.ds(to, depth), :], sems.at[1]).start()
    for i in range(6):
        to = bv.at[i * part : (i + 1) * part, :]
        source = before.at[i * 2 * part + prompt * part : i * 2 * part + (prompt + 1) * part, :]
        pltpu.make_async_copy(source, to, sems.at[2]).start()
    for i in range(2):
        to = here.at[i * part : (i + 1) * part, :]
        pltpu.make_async_copy(xs[6 + i].at[mine, here_columns], to, sems.at[3]).start()
    start_shards(ws[:4], w_at, wh, sems.at[4])
    pltpu.make_async_copy(there, there, sems.at[0]).wait()
    pltpu.make_async_copy(wt, wt, sems.at[1]).wait()
    cols = acc.shape[1]
    for n in range(cols // 256):
        at = slice(n * 256, n * 256 + 256)
        acc[:, at] = jnp.dot(there[...], wt[:, at], preferred_element_type=F32)
    pltpu.make_async_copy(bv, bv, sems.at[2]).wait()
    acc[: 6 * part, :] += bv[...]
    pltpu.make_async_copy(here, here, sems.at[3]).wait()
    pltpu.make_async_copy(wh, wh, sems.at[4]).wait()
    for n in range(cols // 256):
        at = slice(n * 256, n * 256 + 256)
        acc[6 * part :, at] += jnp.dot(here[...], wh[:, at], preferred_element_type=F32)
    for i in range(8):
        for r in range(2):
            to = pl.multiple_of(x_at[i] * 32 + r * (o_ref.shape[0] // 2), 32)
            o_ref[pl.ds(to, 32), :] = acc[i * part + r * 32 : i * part + r * 32 + 32, :]


def project(prompt, rows, x_at, shards, w_at, before):
    span, wide = rows[0].shape[0] * 4, rows[0].shape[1] // 2
    cols = shards[0].shape[1]
    return pl.pallas_call(
        functools.partial(project_kernel, prompt),
        in_specs=[smem()] * 2 + [hbm()] * 17,
        out_specs=vmem(),
        out_shape=jax.ShapeDtypeStruct((span, cols), F32),
        scratch_shapes=[
            pltpu.VMEM((span, wide), BF),
            pltpu.VMEM((span // 4, wide), BF),
            pltpu.VMEM((span // 4 * 3, cols), F32),
            pltpu.VMEM((wide, cols), BF),
            pltpu.VMEM((wide, cols), BF),
            pltpu.VMEM((span, cols), F32),
            pltpu.SemaphoreType.DMA((5,)),
        ],
        compiler_params=pltpu.CompilerParams(vmem_limit_bytes=60 * MB),
        cost_estimate=pl.CostEstimate(flops=MB, bytes_accessed=MB, transcendentals=0),
        name="project",
    )(x_at, w_at, *rows, *shards, before)


def rotate_kernel(rot_scale, owner_ref, a_ref, b_ref, cos_ref, sin_ref, q_ref, k_ref, v_ref, p_ref):
    cos, sin = cos_ref[...], sin_ref[...]
    heads = q_ref.shape[0]

    def total(j):
        at = slice(j * 128, (j + 1) * 128)
        return a_ref[:, at] + b_ref[:, at]

    def rotated(j):
        part = total(j)
        return part * cos + pltpu.roll(part, 64, 1) * sin

    for j in range(heads):
        q_ref[j] = (rotated(j) * rot_scale).astype(BF)
    keys = rotated(heads).astype(BF)
    values = total(heads + 1).astype(BF)
    half = keys.shape[0] // 2
    for s in range(half // 32):
        for r in range(2):
            rows = slice(r * half + s * 32, r * half + s * 32 + 32)
            to = slice(s * 64 + r * 32, s * 64 + r * 32 + 32)
            k_ref[to, :] = keys[rows]
            v_ref[to, :] = values[rows]
    count = owner_ref.shape[1]
    page = k_ref.shape[0] // count
    p_ref[...] = jnp.zeros_like(p_ref)
    body = CAP * 2 * page
    line = lax.broadcasted_iota(jnp.int32, (16, 128), 0)
    for p in range(count):
        owner = owner_ref[0, p]
        rank = jnp.int32(0)
        for q in range(p):
            rank += (owner_ref[0, q] == owner).astype(jnp.int32)
        marks = jnp.where(line == 2 * CAP + rank, p + 1.0, 0.0)
        for c, ref in enumerate((k_ref, v_ref)):
            part = ref[p * page : (p + 1) * page, :].astype(F32)
            most = jnp.max(jnp.max(jnp.abs(part), axis=0, keepdims=True), axis=1, keepdims=True)
            scale = (most + 1e-06).astype(BF).astype(F32)
            at = pl.multiple_of((rank * 2 + c) * page, page)
            p_ref[owner, pl.ds(at, page), :] = (part / scale).astype(BF)
            marks = jnp.where(line == rank * 2 + c, scale, marks)
        p_ref[owner, body:, :] = (p_ref[owner, body:, :].astype(F32) + marks).astype(BF)


def rotate(own, got, cosine, sine, page_owner, groups):
    span, cols = own.shape
    heads = cols // 128 - 2
    page = span // page_owner.shape[1]
    scale = math.log2(math.e) / math.sqrt(128)
    return pl.pallas_call(
        functools.partial(rotate_kernel, scale),
        in_specs=[smem()] + [vmem()] * 4,
        out_specs=[vmem()] * 4,
        out_shape=[
            jax.ShapeDtypeStruct((heads, span, 128), BF),
            jax.ShapeDtypeStruct((span, 128), BF),
            jax.ShapeDtypeStruct((span, 128), BF),
            jax.ShapeDtypeStruct((groups, CAP * 2 * page + 16, 128), BF),
        ],
        compiler_params=pltpu.CompilerParams(vmem_limit_bytes=60 * MB),
        name="rotate",
    )(page_owner, own, got, cosine, sine)


def attend_kernel(chunk, block, live_ref, q_ref, k_hbm, v_hbm, kn_ref, vn_ref, o_ref, k_ref, v_ref, sems):
    live = live_ref[0]
    blocks = k_ref.shape[0] // block
    head = pl.program_id(0)

    def loads(j):
        at = pl.ds(pl.multiple_of(j * block, block), block)
        return (
            pltpu.make_async_copy(k_hbm.at[at, :], k_ref.at[at, :], sems.at[0, j]),
            pltpu.make_async_copy(v_hbm.at[at, :], v_ref.at[at, :], sems.at[1, j]),
        )

    @pl.when(head == 0)
    def _():
        for j in range(blocks):
            for load in loads(j):
                load.start()

    q = q_ref[0]
    full = live // block
    left = live - full * block

    def scores(keys, allowed):
        s = lax.dot_general(q, keys, (((1,), (1,)), ((), ())), preferred_element_type=F32)
        return s if allowed is None else jnp.where(allowed(s.shape), s, -1e30)

    def lanes(op, values):
        return functools.reduce(
            op, [values[:, c * 128 : (c + 1) * 128] for c in range(values.shape[1] // 128)]
        )

    def weigh(s, top, values):
        p = jnp.exp2(s - top)
        return lanes(jnp.add, p), jnp.dot(p.astype(BF), values, preferred_element_type=F32)

    def part(j):
        at = pl.ds(pl.multiple_of(j * block, block), block)
        return k_ref[at, :], v_ref[at, :]

    def arrive(j):
        @pl.when(head == 0)
        def _():
            for load in loads(j):
                load.wait()

    def part_allowed(shape):
        return lax.broadcasted_iota(jnp.int32, shape, 1) < left

    def new_allowed(shape):
        i = lax.broadcasted_iota(jnp.int32, shape, 0)
        row = i // 32 * 64 + chunk * 32 + i % 32
        return lax.broadcasted_iota(jnp.int32, shape, 1) <= row

    def every(one, state, await_block):
        def body(j, state):
            await_block(j)
            return one(state, *part(j), None)

        state = lax.fori_loop(1, full, body, state)

        def rest(j, carry):
            await_block(j)
            return carry

        lax.fori_loop(full, blocks, rest, 0)
        state = lax.cond(
            left > 0, lambda st: one(st, *part(full), part_allowed), lambda st: st, state
        )
        return one(state, kn_ref[...], vn_ref[...], new_allowed)

    def finish(total, out):
        o_ref[...] = (out / jnp.sum(total, axis=1, keepdims=True)).astype(BF)

    arrive(0)
    keys, values = part(0)
    s = scores(keys, None)
    first_top = jnp.max(s, axis=1, keepdims=True)
    first = weigh(s, first_top, values)

    def fixed(state, keys, values, allowed):
        most, total, out = state
        s = scores(keys, allowed)
        more, term = weigh(s, first_top, values)
        return jnp.maximum(most, lanes(jnp.maximum, s)), total + more, out + term

    start = jnp.broadcast_to(first_top, (q.shape[0], 128))
    most, total, out = every(fixed, (start, *first), arrive)
    finish(total, out)

    @pl.when(jnp.max(most - first_top) > 40.0)
    def _():
        def running(state, keys, values, allowed):
            top, total, out = state
            s = scores(keys, allowed)
            new_top = jnp.maximum(top, jnp.max(s, axis=1, keepdims=True))
            more, term = weigh(s, new_top, values)
            keep = jnp.exp2(top - new_top)
            return new_top, total * keep + more, out * keep + term

        _, total, out = every(running, (first_top, *first), lambda j: None)
        finish(total, out)


def attend(chunk, q, cache_k, cache_v, keys, values, live):
    heads, span, width = q.shape
    rows = span // 2
    prefix = cache_k.shape[0]
    block = 2048
    return pl.pallas_call(
        functools.partial(attend_kernel, chunk, block),
        grid=(heads,),
        in_specs=[
            smem(),
            pl.BlockSpec((1, rows, width), lambda i: (i, chunk, 0)),
            hbm(),
            hbm(),
            vmem(),
            vmem(),
        ],
        out_specs=pl.BlockSpec((rows, width), lambda i: (0, i)),
        out_shape=jax.ShapeDtypeStruct((rows, heads * width), BF),
        scratch_shapes=[
            pltpu.VMEM((prefix, width), BF),
            pltpu.VMEM((prefix, width), BF),
            pltpu.SemaphoreType.DMA((2, prefix // block)),
        ],
        compiler_params=pltpu.CompilerParams(vmem_limit_bytes=60 * MB),
        cost_estimate=pl.CostEstimate(flops=MB, bytes_accessed=MB, transcendentals=0),
        name="attend",
    )(live, q, cache_k, cache_v, keys, values)


def output_kernel(x_at, a0, a1, a2, a3, mine, other, o_ref, xv, wv, xsem, wsem):
    shards, depth, cols = wv.shape
    core = x_at[4]
    width = a0.shape[1]
    copies = []
    for i, ref in enumerate((a0, a1, a2, a3)):
        to = pl.multiple_of(x_at[i] * width, width)
        copies.append(pltpu.make_async_copy(ref, xv.at[:, pl.ds(to, width)], xsem.at[i]))
    for copy in copies:
        copy.start()
    for k in range(shards // 2):
        sem = wsem.at[k // 2]
        pltpu.make_async_copy(mine.at[k], wv.at[2 * k + core], sem).start()
        pltpu.make_async_copy(other.at[k], wv.at[2 * k + 1 - core], sem).start()
    for copy in copies:
        copy.wait()
    for i in range(shards // 4):
        group = wv.at[4 * i : 4 * i + 4]
        pltpu.make_async_copy(group, group, wsem.at[i]).wait()
        w = jnp.concatenate([wv[j] for j in range(4 * i, 4 * i + 4)], axis=1)
        o_ref[:, 4 * i * cols : 4 * (i + 1) * cols] = jnp.dot(
            xv[...], w, preferred_element_type=F32
        ).astype(BF)


def output(pieces, weights, x, core):
    rows, width = pieces[0].shape
    x_at = jnp.stack([x, (x + 3) % 4, (x + 1) % 4, (x + 2) % 4, core]).astype(jnp.int32)
    shards, depth, cols = weights[0].shape
    shards = 2 * shards
    return pl.pallas_call(
        output_kernel,
        in_specs=[smem()] + [hbm()] * 6,
        out_specs=vmem(),
        out_shape=jax.ShapeDtypeStruct((rows, shards * cols), BF),
        scratch_shapes=[
            pltpu.VMEM((rows, 4 * width), BF),
            pltpu.VMEM((shards, depth, cols), BF),
            pltpu.SemaphoreType.DMA((4,)),
            pltpu.SemaphoreType.DMA((4,)),
        ],
        compiler_params=pltpu.CompilerParams(vmem_limit_bytes=60 * MB),
        cost_estimate=pl.CostEstimate(flops=MB, bytes_accessed=MB, transcendentals=0),
        name="output",
    )(x_at, *pieces, *weights)


def finish_kernel(*refs):
    o_ref = refs[-1]
    for r, ref in enumerate(refs[:-1]):
        for x in range(4):
            total = ref[x].astype(F32) + ref[4 + x].astype(F32)
            total = total.astype(BF)
            for d in range(16):
                to = d * 512 + x * 128
                o_ref[r * 32 : r * 32 + 32, to : to + 128] = total[:, d * 128 : d * 128 + 128]


def finish(parts):
    rows = parts[0].shape[1] * len(parts)
    return pl.pallas_call(
        finish_kernel,
        in_specs=[vmem()] * len(parts),
        out_specs=vmem(),
        out_shape=jax.ShapeDtypeStruct((rows, parts[0].shape[2] * 4), BF),
        compiler_params=pltpu.CompilerParams(vmem_limit_bytes=60 * MB),
        name="finish",
    )(*parts)


def placed_pages(got):
    groups, rows, width = got.shape
    body = rows - 16
    pages = got[:, :body].reshape(1, groups * CAP, 2, body // (2 * CAP), width)
    scales = got[:, body : body + 2 * CAP, 0].reshape(1, groups * CAP, 2, 1)
    ids = got[:, body + 2 * CAP : body + 3 * CAP, 0].astype(jnp.int32) - 1
    return pages, scales, ids.reshape(1, groups * CAP)


def rope_tables(positions, width):
    half = width // 2
    steps = jnp.arange(half, dtype=F32) * (2.0 / width)
    freqs = jnp.exp(-math.log(THETA) * steps)
    angles = positions.astype(F32)[:, None] * freqs[None, :]
    cosine, sine = jnp.cos(angles), jnp.sin(angles)
    return (
        jnp.concatenate([cosine, cosine], axis=1),
        jnp.concatenate([-sine, sine], axis=1),
    )


def body(
    hidden_in, norm_gain, w_query, w_key, w_value, w_out, cache_k, cache_v, prefix_len, page_owner
):
    t, d = lax.axis_index("tensor"), lax.axis_index("decode")
    z, x = t // 4, t % 4
    zh, y, core = d // 8, d // 2 % 4, d % 2
    span = hidden_in.shape[1] * 8
    width = cache_k.shape[-1]
    i = jnp.arange(span, dtype=jnp.int32)
    true_row = i % (span // 2) // 32 * 64 + i // (span // 2) * 32 + i % 32
    tables = rope_tables(prefix_len[0] + true_row, width)
    keep, send, w, *quarters = prepare(
        hidden_in[0], norm_gain, w_query, w_key, w_value, w_out, core, x
    )
    moves = (X_UP, X_FAR, X_DOWN)
    quarters = [quarters[0]] + [to_t(a, pairs) for a, pairs in zip(quarters[1:], moves)]
    chip_rows = jnp.concatenate([keep, to_d(send, CORE_SWAP)], axis=0)
    chip_rows, *quarters = together(chip_rows, *quarters)
    out = stack_out([quarters[i] for i in (0, 3, 2, 1)], x)
    x_at = row_sources(z, x).astype(jnp.int32)
    w_at = shard_sources(zh, y).astype(jnp.int32)
    rows, shards, before, (cosine, sine), out = gather_inputs(chip_rows, w, w_at, out, tables)
    out = lax.all_to_all(out, "decode", 0, 0, axis_index_groups=PARITIES, tiled=True)
    other = project(1, rows, x_at, shards, w_at, before)
    own = project(0, rows, x_at, shards, w_at, after(before, other))
    queries, keys, values, sent = rotate(
        own, to_d(other, CORE_SWAP), cosine, sine, page_owner, 16
    )

    def attend_chunk(chunk, queries):
        return attend(chunk, queries, cache_k[0, 0], cache_v[0, 0], keys, values, prefix_len)

    def spread(attended):
        return [attended] + [to_t(attended, pairs) for pairs in (X_UP, X_DOWN, X_FAR)]

    def back(partial):
        got = lax.all_to_all(partial, "tensor", 0, 0, tiled=True)
        return got.reshape(8, 32, partial.shape[1])

    first = attend_chunk(0, queries)
    first_pieces = spread(first)
    queries, sent, out = together(queries, sent, out, first)[:3]
    out_weights = out, to_d(out, CORE_SWAP)
    got = lax.all_to_all(sent, "decode", 0, 0, tiled=True)
    second = attend_chunk(1, queries)
    second = after(second, out_weights[1])
    first_pieces[0] = after(first_pieces[0], second)
    second_pieces = spread(second)
    first_partial = output(first_pieces, out_weights, x, core)
    first_partial, *second_pieces = together(first_partial, *second_pieces)
    first_back = back(after(first_partial, got))
    second_partial = output(second_pieces, out_weights, x, core)
    first_back = after(first_back, second_partial)
    second_back = back(after(second_partial, first_back))
    attn_out = finish([first_back, second_back])[None]
    return (attn_out, *placed_pages(got))


def solution(mesh):
    in_specs = (
        P("decode", "tensor", None),
        P(),
        P("decode", "tensor"),
        P("decode", "tensor"),
        P("decode", "tensor"),
        P("tensor", "decode"),
        P("decode", "tensor", None, None),
        P("decode", "tensor", None, None),
        P("decode"),
        P("decode", None),
    )
    out_specs = (
        P("decode", "tensor", None),
        P("decode", None, None, None, "tensor"),
        P("decode", None, None, "tensor"),
        P("decode", None),
    )
    return jax.shard_map(body, mesh=mesh, in_specs=in_specs, out_specs=out_specs, check_vma=False)
```

```python
import functools
import math

import jax
import jax.numpy as jnp
from jax import lax
from jax.experimental import pallas as pl
from jax.experimental.pallas import tpu as pltpu
from jax.sharding import PartitionSpec as P

CAP = 2
THETA = 500000.0
EPS = 1e-05
BF = jnp.bfloat16
F32 = jnp.float32
MB = 2**20


def tensor_perm(move):
    pairs = []
    for z in range(2):
        for x in range(4):
            a, b = move(z, x)
            pairs.append((z * 4 + x, a * 4 + b % 4))
    return pairs


def decode_perm(move):
    pairs = []
    for z in range(2):
        for y in range(4):
            for c in range(2):
                a, b, e = move(z, y, c)
                pairs.append((z * 8 + y * 2 + c, a * 8 + (b % 4) * 2 + e))
    return pairs


X_UP = tensor_perm(lambda z, x: (z, x + 1))
X_DOWN = tensor_perm(lambda z, x: (z, x - 1))
Z_SWAP = tensor_perm(lambda z, x: (1 - z, x))
Y_UP = decode_perm(lambda z, y, c: (z, y + 1, c))
Y_DOWN = decode_perm(lambda z, y, c: (z, y - 1, c))
Y_FAR = decode_perm(lambda z, y, c: (z, y + 2, c))
ZH_SWAP = decode_perm(lambda z, y, c: (1 - z, y, c))
CORE_SWAP = decode_perm(lambda z, y, c: (z, y, 1 - c))
PARITIES = [list(range(c, 16, 2)) for c in range(2)]
X_FAR = tensor_perm(lambda z, x: (z, x + 2))


def to_t(value, pairs):
    return lax.ppermute(value, "tensor", pairs)


def to_d(value, pairs):
    return lax.ppermute(value, "decode", pairs)


def after(value, *others):
    return lax.optimization_barrier((value, *others))[0]


def together(*values):
    return lax.optimization_barrier(values)


def gather_inputs(rows, w, w_at, out, tables):
    low, high = to_d(w, Y_UP), to_d(w, Y_DOWN)
    left, right, over = to_t(rows, X_UP), to_t(rows, X_DOWN), to_t(rows, Z_SWAP)
    low, high, left, right, over = together(low, high, left, right, over)
    w_over = to_d(after(w, low), ZH_SWAP)
    far_low = to_d(low, Y_UP)
    far = to_t(left, X_UP)
    over_right = to_t(over, X_DOWN)
    far, over_right, w_over, far_low, out, *tables = together(
        far, over_right, w_over, far_low, out, *tables
    )
    over_left = to_t(after(over, far), X_UP)
    over_far = to_t(over_right, X_DOWN)
    over_low, over_high = to_d(w_over, Y_UP), to_d(w_over, Y_DOWN)
    far_over = to_d(far_low, ZH_SWAP)
    early = [rows, left, right, far, over, over_right]
    here = [w, low, high, far_low]
    before = project_early(early, here, w_at)
    over_left, over_far, over_low, over_high, far_over, before, out = together(
        over_left, over_far, over_low, over_high, far_over, before, out
    )
    return (
        early + [over_left, over_far],
        here + [w_over, over_low, over_high, far_over],
        before,
        tables,
        out,
    )


def row_sources(z, x):
    here, there = z * 4, (1 - z) * 4
    lo, hi, end = (x + 3) % 4, (x + 1) % 4, (x + 2) % 4
    places = [here + at for at in (x, lo, hi, end)] + [there + at for at in (x, hi, lo, end)]
    return jnp.stack(places)


def shard_sources(zh, y):
    here, there = zh * 4, (1 - zh) * 4
    lo, hi, end = (y + 3) % 4, (y + 1) % 4, (y + 2) % 4
    return jnp.stack([first + at for first in (here, there) for at in (y, lo, hi, end)])


def stack_out(pieces, x):
    depth, wide = pieces[0].shape

    def kernel(x_ref, a0, a1, a2, a3, o_ref):
        for i, ref in enumerate((a0, a1, a2, a3)):
            to = pl.multiple_of((x_ref[0] + i) % 4 * depth, depth)
            for k in range(8):
                o_ref[k, pl.ds(to, depth), :] = ref[...]

    return pl.pallas_call(
        kernel,
        in_specs=[smem()] + [vmem()] * 4,
        out_specs=vmem(),
        out_shape=jax.ShapeDtypeStruct((8, 4 * depth, wide), BF),
        compiler_params=pltpu.CompilerParams(vmem_limit_bytes=20 * MB),
        name="stack",
    )(x[None].astype(jnp.int32), *pieces)


def hbm():
    return pl.BlockSpec(memory_space=pltpu.HBM)


def vmem():
    return pl.BlockSpec(memory_space=pltpu.VMEM)


def smem():
    return pl.BlockSpec(memory_space=pltpu.SMEM)


def prepare_kernel(at_ref, h_ref, gain_ref, wq, wk, wv, wo, keep_ref, send_ref, w_ref, *parts):
    q_cols, k_cols = wq.shape[1], wk.shape[1]
    w_ref[:, :q_cols] = wq[...]
    w_ref[:, q_cols : q_cols + k_cols] = wk[...]
    w_ref[:, q_cols + k_cols :] = wv[...]
    rows, width = h_ref.shape
    depth = wq.shape[0]
    even_core = at_ref[0] == 0
    wide = wo.shape[1] // 4
    for j, part in enumerate(parts):
        to = pl.multiple_of((at_ref[1] + j) % 4 * wide, wide)
        part[...] = wo[:, pl.ds(to, wide)]

    def step(i, carry):
        at = pl.ds(pl.multiple_of(i * 16, 16), 16)
        h = h_ref[at, :].astype(F32)
        mean_sq = jnp.sum(h * h, axis=1, keepdims=True) / width
        normed = (h * lax.rsqrt(mean_sq + EPS) * gain_ref[...]).astype(BF)
        for k in range(width // (2 * depth)):
            even = normed[:, 2 * k * depth : (2 * k + 1) * depth]
            odd = normed[:, (2 * k + 1) * depth : (2 * k + 2) * depth]
            keep_ref[at, k * depth : (k + 1) * depth] = jnp.where(even_core, even, odd)
            send_ref[at, k * depth : (k + 1) * depth] = jnp.where(even_core, odd, even)
        return carry

    lax.fori_loop(0, rows // 16, step, 0)


def prepare(hidden, gain, w_query, w_key, w_value, w_out, core, x):
    rows, width = hidden.shape
    depth = w_query.shape[0]
    cols = w_query.shape[1] + 2 * w_key.shape[1]
    return pl.pallas_call(
        prepare_kernel,
        in_specs=[smem()] + [vmem()] * 6,
        out_specs=[vmem()] * 7,
        out_shape=[
            jax.ShapeDtypeStruct((rows, width // 2), BF),
            jax.ShapeDtypeStruct((rows, width // 2), BF),
            jax.ShapeDtypeStruct((depth, cols), BF),
        ]
        + [jax.ShapeDtypeStruct((w_out.shape[0], w_out.shape[1] // 4), BF)] * 4,
        compiler_params=pltpu.CompilerParams(vmem_limit_bytes=60 * MB),
        name="prepare",
    )(jnp.stack([core, x]).astype(jnp.int32), hidden, gain[None], w_query, w_key, w_value, w_out)


def start_shards(refs, w_at, wv, sem):
    for i, ref in enumerate(refs):
        depth = ref.shape[0]
        to = pl.multiple_of(w_at[i] % 4 * depth, depth)
        pltpu.make_async_copy(ref, wv.at[pl.ds(to, depth), :], sem).start()


def project_early_kernel(w_at, *refs):
    xs, ws = refs[:6], refs[6:10]
    o_ref, xv, wv, xsem, wsem = refs[10:]
    rows, wide = xs[0].shape[0], xv.shape[1]
    columns = pl.ds(pl.multiple_of(w_at[0] // 4 * wide, wide), wide)
    for i, ref in enumerate(xs):
        to = xv.at[i * rows : (i + 1) * rows, :]
        pltpu.make_async_copy(ref.at[:, columns], to, xsem).start()
    start_shards(ws, w_at, wv, wsem)
    pltpu.make_async_copy(xv, xv, xsem).wait()
    pltpu.make_async_copy(wv, wv, wsem).wait()
    for n in range(o_ref.shape[1] // 256):
        at = slice(n * 256, n * 256 + 256)
        o_ref[:, at] = jnp.dot(xv[...], wv[:, at], preferred_element_type=F32)


def project_early(rows, shards, w_at):
    n = len(rows) * rows[0].shape[0]
    wide, cols = rows[0].shape[1] // 2, shards[0].shape[1]
    return pl.pallas_call(
        project_early_kernel,
        in_specs=[smem()] + [hbm()] * 10,
        out_specs=vmem(),
        out_shape=jax.ShapeDtypeStruct((n, cols), F32),
        scratch_shapes=[
            pltpu.VMEM((n, wide), BF),
            pltpu.VMEM((wide, cols), BF),
            pltpu.SemaphoreType.DMA,
            pltpu.SemaphoreType.DMA,
        ],
        compiler_params=pltpu.CompilerParams(vmem_limit_bytes=60 * MB),
        cost_estimate=pl.CostEstimate(flops=1, bytes_accessed=1, transcendentals=0),
        name="project_early",
    )(w_at, *rows, *shards)


def project_kernel(prompt, x_at, w_at, *refs):
    xs, ws, before = refs[:8], refs[8:16], refs[16]
    o_ref, there, here, bv, wt, wh, acc, sems = refs[17:]
    wide = there.shape[1]
    part = o_ref.shape[0] // 8
    mine = pl.ds(prompt * part, part)
    side = w_at[0] // 4
    here_columns = pl.ds(pl.multiple_of(side * wide, wide), wide)
    there_columns = pl.ds(pl.multiple_of((1 - side) * wide, wide), wide)
    for i, ref in enumerate(xs):
        to = there.at[i * part : (i + 1) * part, :]
        pltpu.make_async_copy(ref.at[mine, there_columns], to, sems.at[0]).start()
    for i, ref in enumerate(ws[4:]):
        depth = ref.shape[0]
        to = pl.multiple_of(w_at[4 + i] % 4 * depth, depth)
        pltpu.make_async_copy(ref, wt.at[pl.ds(to, depth), :], sems.at[1]).start()
    for i in range(6):
        to = bv.at[i * part : (i + 1) * part, :]
        source = before.at[i * 2 * part + prompt * part : i * 2 * part + (prompt + 1) * part, :]
        pltpu.make_async_copy(source, to, sems.at[2]).start()
    for i in range(2):
        to = here.at[i * part : (i + 1) * part, :]
        pltpu.make_async_copy(xs[6 + i].at[mine, here_columns], to, sems.at[3]).start()
    start_shards(ws[:4], w_at, wh, sems.at[4])
    pltpu.make_async_copy(there, there, sems.at[0]).wait()
    pltpu.make_async_copy(wt, wt, sems.at[1]).wait()
    cols = acc.shape[1]
    for n in range(cols // 256):
        at = slice(n * 256, n * 256 + 256)
        acc[:, at] = jnp.dot(there[...], wt[:, at], preferred_element_type=F32)
    pltpu.make_async_copy(bv, bv, sems.at[2]).wait()
    acc[: 6 * part, :] += bv[...]
    pltpu.make_async_copy(here, here, sems.at[3]).wait()
    pltpu.make_async_copy(wh, wh, sems.at[4]).wait()
    for n in range(cols // 256):
        at = slice(n * 256, n * 256 + 256)
        acc[6 * part :, at] += jnp.dot(here[...], wh[:, at], preferred_element_type=F32)
    for i in range(8):
        for r in range(2):
            to = pl.multiple_of(x_at[i] * 32 + r * (o_ref.shape[0] // 2), 32)
            o_ref[pl.ds(to, 32), :] = acc[i * part + r * 32 : i * part + r * 32 + 32, :]


def project(prompt, rows, x_at, shards, w_at, before):
    span, wide = rows[0].shape[0] * 4, rows[0].shape[1] // 2
    cols = shards[0].shape[1]
    return pl.pallas_call(
        functools.partial(project_kernel, prompt),
        in_specs=[smem()] * 2 + [hbm()] * 17,
        out_specs=vmem(),
        out_shape=jax.ShapeDtypeStruct((span, cols), F32),
        scratch_shapes=[
            pltpu.VMEM((span, wide), BF),
            pltpu.VMEM((span // 4, wide), BF),
            pltpu.VMEM((span // 4 * 3, cols), F32),
            pltpu.VMEM((wide, cols), BF),
            pltpu.VMEM((wide, cols), BF),
            pltpu.VMEM((span, cols), F32),
            pltpu.SemaphoreType.DMA((5,)),
        ],
        compiler_params=pltpu.CompilerParams(vmem_limit_bytes=60 * MB),
        cost_estimate=pl.CostEstimate(flops=1, bytes_accessed=1, transcendentals=0),
        name="project",
    )(x_at, w_at, *rows, *shards, before)


def rotate_kernel(rot_scale, a_ref, b_ref, cos_ref, sin_ref, q_ref, k_ref, v_ref):
    cos, sin = cos_ref[...], sin_ref[...]
    heads = q_ref.shape[0]

    def total(j):
        at = slice(j * 128, (j + 1) * 128)
        return a_ref[:, at] + b_ref[:, at]

    def rotated(j):
        part = total(j)
        return part * cos + pltpu.roll(part, 64, 1) * sin

    for j in range(heads):
        q_ref[j] = (rotated(j) * rot_scale).astype(BF)
    keys = rotated(heads).astype(BF)
    values = total(heads + 1).astype(BF)
    half = keys.shape[0] // 2
    for s in range(half // 32):
        for r in range(2):
            rows = slice(r * half + s * 32, r * half + s * 32 + 32)
            to = slice(s * 64 + r * 32, s * 64 + r * 32 + 32)
            k_ref[to, :] = keys[rows]
            v_ref[to, :] = values[rows]


def rotate(own, got, cosine, sine):
    span, cols = own.shape
    heads = cols // 128 - 2
    scale = math.log2(math.e) / math.sqrt(128)
    return pl.pallas_call(
        functools.partial(rotate_kernel, scale),
        in_specs=[vmem()] * 4,
        out_specs=[vmem()] * 3,
        out_shape=[
            jax.ShapeDtypeStruct((heads, span, 128), BF),
            jax.ShapeDtypeStruct((span, 128), BF),
            jax.ShapeDtypeStruct((span, 128), BF),
        ],
        compiler_params=pltpu.CompilerParams(vmem_limit_bytes=60 * MB),
        name="rotate",
    )(own, got, cosine, sine)


def attend_kernel(
    chunk, block, live_ref, q_ref, k_hbm, v_hbm, kn_ref, vn_ref, o_ref, k_ref, v_ref, sa, sb,
    total_ref, out_ref, sems
):
    heads, rows, width = q_ref.shape
    live = live_ref[0]
    blocks = k_ref.shape[0] // block
    q = q_ref[...].reshape(heads * rows, width)
    full = live // block
    left = live - full * block

    def loads(j):
        at = pl.ds(pl.multiple_of(j * block, block), block)
        return (
            pltpu.make_async_copy(k_hbm.at[at, :], k_ref.at[at, :], sems.at[0, j]),
            pltpu.make_async_copy(v_hbm.at[at, :], v_ref.at[at, :], sems.at[1, j]),
        )

    for j in range(blocks):
        for load in loads(j):
            load.start()

    def arrive(j):
        for load in loads(j):
            load.wait()

    def part(ref, j):
        return ref[pl.ds(pl.multiple_of(j * block, block), block), :]

    def scores(keys):
        return lax.dot_general(q, keys, (((1,), (1,)), ((), ())), preferred_element_type=F32)

    def lanes(values):
        return functools.reduce(
            jnp.add, [values[:, c * 128 : (c + 1) * 128] for c in range(values.shape[1] // 128)]
        )

    def weigh(s, top, values):
        p = jnp.exp2(s - top)
        return lanes(p), jnp.dot(p.astype(BF), values, preferred_element_type=F32)

    def add(s, top, values):
        more, term = weigh(s, top, values)
        total_ref[...] += more
        out_ref[...] += term

    def finish():
        r = (out_ref[...] / jnp.sum(total_ref[...], axis=1, keepdims=True)).astype(BF)
        for h in range(heads):
            o_ref[:, h * width : (h + 1) * width] = r[h * rows : (h + 1) * rows]

    def masked_part():
        s = scores(part(k_ref, full))
        return jnp.where(lax.broadcasted_iota(jnp.int32, s.shape, 1) < left, s, -1e30)

    def masked_new():
        s = scores(kn_ref[...])
        i = lax.broadcasted_iota(jnp.int32, s.shape, 0) % rows
        row = i // 32 * 64 + chunk * 32 + i % 32
        return jnp.where(lax.broadcasted_iota(jnp.int32, s.shape, 1) <= row, s, -1e30)

    arrive(0)
    sa[...] = scores(part(k_ref, 0))
    top = jnp.max(sa[...], axis=1, keepdims=True)
    total_ref[...] = jnp.zeros_like(total_ref)
    out_ref[...] = jnp.zeros_like(out_ref)

    def pair(i, carry):
        arrive(2 * i + 1)
        after = jnp.minimum(2 * i + 2, blocks - 1)

        @pl.when(2 * i + 2 < blocks)
        def _():
            arrive(2 * i + 2)

        sb[...] = scores(part(k_ref, 2 * i + 1))
        add(sa[...], top, part(v_ref, 2 * i))
        sa[...] = scores(part(k_ref, after))
        add(sb[...], top, part(v_ref, 2 * i + 1))
        return carry

    lax.fori_loop(0, full // 2, pair, 0)

    def rest(j, carry):
        arrive(j)
        return carry

    lax.fori_loop(full // 2 * 2 + 1, blocks, rest, 0)

    @pl.when(full % 2 == 1)
    def _():
        add(sa[...], top, part(v_ref, full - 1))

    @pl.when(left > 0)
    def _():
        add(masked_part(), top, part(v_ref, full))

    add(masked_new(), top, vn_ref[...])
    finish()

    @pl.when(jnp.max(total_ref[...]) > 2.0**40)
    def _():
        def running(top, s, values):
            new_top = jnp.maximum(top, jnp.max(s, axis=1, keepdims=True))
            keep = jnp.exp2(top - new_top)
            more, term = weigh(s, new_top, values)
            total_ref[...] = total_ref[...] * keep + more
            out_ref[...] = out_ref[...] * keep + term
            return new_top

        total_ref[...] = jnp.zeros_like(total_ref)
        out_ref[...] = jnp.zeros_like(out_ref)

        def body(j, top):
            return running(top, scores(part(k_ref, j)), part(v_ref, j))

        top_now = lax.fori_loop(0, full, body, top)
        top_now = lax.cond(
            left > 0, lambda t: running(t, masked_part(), part(v_ref, full)), lambda t: t, top_now
        )
        running(top_now, masked_new(), vn_ref[...])
        finish()

def attend(chunk, q, cache_k, cache_v, keys, values, live):
    heads, span, width = q.shape
    rows = span // 2
    prefix = cache_k.shape[0]
    block = 1024
    return pl.pallas_call(
        functools.partial(attend_kernel, chunk, block),
        grid=(1,),
        in_specs=[
            smem(),
            pl.BlockSpec((heads, rows, width), lambda i: (0, chunk, 0)),
            hbm(),
            hbm(),
            vmem(),
            vmem(),
        ],
        out_specs=pl.BlockSpec((rows, heads * width), lambda i: (0, 0)),
        out_shape=jax.ShapeDtypeStruct((rows, heads * width), BF),
        scratch_shapes=[
            pltpu.VMEM((prefix, width), BF),
            pltpu.VMEM((prefix, width), BF),
            pltpu.VMEM((heads * rows, block), F32),
            pltpu.VMEM((heads * rows, block), F32),
            pltpu.VMEM((heads * rows, 128), F32),
            pltpu.VMEM((heads * rows, width), F32),
            pltpu.SemaphoreType.DMA((2, prefix // block)),
        ],
        compiler_params=pltpu.CompilerParams(vmem_limit_bytes=60 * MB),
        cost_estimate=pl.CostEstimate(flops=1, bytes_accessed=1, transcendentals=0),
        name="attend",
    )(live, q, cache_k, cache_v, keys, values)


def output_kernel(x_at, a0, a1, a2, a3, mine, other, o_ref, xv, wv, xsem, wsem):
    shards, depth, cols = wv.shape
    core = x_at[4]
    width = a0.shape[1]
    copies = []
    for i, ref in enumerate((a0, a1, a2, a3)):
        to = pl.multiple_of(x_at[i] * width, width)
        copies.append(pltpu.make_async_copy(ref, xv.at[:, pl.ds(to, width)], xsem.at[i]))
    for copy in copies:
        copy.start()
    for k in range(shards // 2):
        sem = wsem.at[k // 2]
        pltpu.make_async_copy(mine.at[k], wv.at[2 * k + core], sem).start()
        pltpu.make_async_copy(other.at[k], wv.at[2 * k + 1 - core], sem).start()
    for copy in copies:
        copy.wait()
    for i in range(shards // 4):
        group = wv.at[4 * i : 4 * i + 4]
        pltpu.make_async_copy(group, group, wsem.at[i]).wait()
        w = jnp.concatenate([wv[j] for j in range(4 * i, 4 * i + 4)], axis=1)
        o_ref[:, 4 * i * cols : 4 * (i + 1) * cols] = jnp.dot(
            xv[...], w, preferred_element_type=F32
        ).astype(BF)


def output(pieces, weights, x, core):
    rows, width = pieces[0].shape
    x_at = jnp.stack([x, (x + 3) % 4, (x + 1) % 4, (x + 2) % 4, core]).astype(jnp.int32)
    shards, depth, cols = weights[0].shape
    shards = 2 * shards
    return pl.pallas_call(
        output_kernel,
        in_specs=[smem()] + [hbm()] * 6,
        out_specs=vmem(),
        out_shape=jax.ShapeDtypeStruct((rows, shards * cols), BF),
        scratch_shapes=[
            pltpu.VMEM((rows, 4 * width), BF),
            pltpu.VMEM((shards, depth, cols), BF),
            pltpu.SemaphoreType.DMA((4,)),
            pltpu.SemaphoreType.DMA((4,)),
        ],
        compiler_params=pltpu.CompilerParams(vmem_limit_bytes=60 * MB),
        cost_estimate=pl.CostEstimate(flops=1, bytes_accessed=1, transcendentals=0),
        name="output",
    )(x_at, *pieces, *weights)


def finish_kernel(*refs):
    o_ref = refs[-1]
    for r, ref in enumerate(refs[:-1]):
        for x in range(4):
            total = ref[x].astype(F32) + ref[4 + x].astype(F32)
            total = total.astype(BF)
            for d in range(16):
                to = d * 512 + x * 128
                o_ref[r * 32 : r * 32 + 32, to : to + 128] = total[:, d * 128 : d * 128 + 128]


def finish(parts):
    rows = parts[0].shape[1] * len(parts)
    return pl.pallas_call(
        finish_kernel,
        in_specs=[vmem()] * len(parts),
        out_specs=vmem(),
        out_shape=jax.ShapeDtypeStruct((rows, parts[0].shape[2] * 4), BF),
        compiler_params=pltpu.CompilerParams(vmem_limit_bytes=60 * MB),
        name="finish",
    )(*parts)


def place_kernel(page_of, at_ref, *refs):
    sources, (out_ref, scale_ref) = refs[:8], refs[8:]
    page = out_ref.shape[2]

    def slot(s, carry):
        number = page_of[s]
        prompt = s // CAP
        away = (prompt // 2 + 4 - at_ref[1]) % 4
        piece = jnp.where(away == 3, 1, jnp.where(away == 0, 0, away + 1))
        side = (prompt // 8 != at_ref[0]).astype(jnp.int32)
        source = piece + 4 * (prompt % 2 != at_ref[2]).astype(jnp.int32)

        @pl.when(number < 0)
        def _():
            out_ref[s] = jnp.zeros(out_ref.shape[1:], BF)
            scale_ref[s] = jnp.zeros(scale_ref.shape[1:], F32)

        for i, ref in enumerate(sources):

            @pl.when((number >= 0) & (source == i))
            def _(ref=ref):
                at = pl.multiple_of(jnp.maximum(number, 0) * page, page)
                rows = ref[side, pl.ds(at, page), :].astype(F32)
                for c in range(2):
                    part = rows[:, c * 128 : (c + 1) * 128]
                    most = jnp.max(jnp.abs(part), axis=0, keepdims=True)
                    most = jnp.max(most, axis=1, keepdims=True)
                    scale = (most + 1e-06).astype(BF).astype(F32)
                    out_ref[s, c] = (part / scale).astype(BF)
                    scale_ref[s, c : c + 1, :] = jnp.broadcast_to(scale, (1, 128))

        return carry

    lax.fori_loop(0, out_ref.shape[0], slot, 0)


def page_rows(keys, values, page_owner):
    count = page_owner.shape[1]
    marks = jnp.pad(page_owner.astype(BF), ((0, 15), (0, 256 - count)))
    own = jnp.concatenate([jnp.concatenate([keys, values], axis=1), marks], axis=0)
    return own, to_d(own, ZH_SWAP)


def place_pages(sources, count, zh, y, core, d):
    span = sources[0].shape[1] - 16
    order = jnp.arange(count, dtype=jnp.int32)
    prompt = jnp.arange(16)
    away = (prompt // 2 - y) % 4
    piece = jnp.array([0, 2, 3, 1])[away]
    source = piece + 4 * (prompt % 2 != core)
    side = (prompt // 8 != zh).astype(jnp.int32)
    marks = jnp.concatenate([a[:, span, :count] for a in sources]).astype(F32)
    pick = (source * 2 + side)[:, None] == jnp.arange(16)[None, :]
    owners = jnp.sum(jnp.where(pick[:, :, None], marks[None], 0.0), axis=1).astype(jnp.int32)
    same = owners[:, :, None] == owners[:, None, :]
    rank = jnp.sum((same & (order[None, :] < order[:, None])[None]).astype(jnp.int32), axis=2)
    chosen = (owners == d)[:, None, :] & (rank[:, None, :] == jnp.arange(CAP)[None, :, None])
    ids = jnp.max(jnp.where(chosen, order[None, None, :], -1), axis=2).reshape(16 * CAP)
    pages, scales = pl.pallas_call(
        place_kernel,
        in_specs=[smem(), smem()] + [vmem()] * 8,
        out_specs=[vmem()] * 2,
        out_shape=[
            jax.ShapeDtypeStruct((16 * CAP, 2, span // count, 128), BF),
            jax.ShapeDtypeStruct((16 * CAP, 2, 128), F32),
        ],
        compiler_params=pltpu.CompilerParams(vmem_limit_bytes=60 * MB),
        cost_estimate=pl.CostEstimate(flops=1, bytes_accessed=1, transcendentals=0),
        name="place",
    )(ids, jnp.stack([zh, y, core]).astype(jnp.int32), *sources)
    return pages[None], scales[None, :, :, :1].astype(BF), ids[None]


def rope_tables(positions, width):
    half = width // 2
    steps = jnp.arange(half, dtype=F32) * (2.0 / width)
    freqs = jnp.exp(-math.log(THETA) * steps)
    angles = positions.astype(F32)[:, None] * freqs[None, :]
    cosine, sine = jnp.cos(angles), jnp.sin(angles)
    return (
        jnp.concatenate([cosine, cosine], axis=1),
        jnp.concatenate([-sine, sine], axis=1),
    )


def body(
    hidden_in, norm_gain, w_query, w_key, w_value, w_out, cache_k, cache_v, prefix_len, page_owner
):
    t, d = lax.axis_index("tensor"), lax.axis_index("decode")
    z, x = t // 4, t % 4
    zh, y, core = d // 8, d // 2 % 4, d % 2
    span = hidden_in.shape[1] * 8
    width = cache_k.shape[-1]
    i = jnp.arange(span, dtype=jnp.int32)
    true_row = i % (span // 2) // 32 * 64 + i // (span // 2) * 32 + i % 32
    tables = rope_tables(prefix_len[0] + true_row, width)
    keep, send, w, *quarters = prepare(
        hidden_in[0], norm_gain, w_query, w_key, w_value, w_out, core, x
    )
    moves = (X_UP, X_FAR, X_DOWN)
    quarters = [quarters[0]] + [to_t(a, pairs) for a, pairs in zip(quarters[1:], moves)]
    chip_rows = jnp.concatenate([keep, to_d(send, CORE_SWAP)], axis=0)
    chip_rows, *quarters = together(chip_rows, *quarters)
    out = stack_out([quarters[i] for i in (0, 3, 2, 1)], x)
    x_at = row_sources(z, x).astype(jnp.int32)
    w_at = shard_sources(zh, y).astype(jnp.int32)
    rows, shards, before, (cosine, sine), out = gather_inputs(chip_rows, w, w_at, out, tables)
    out = lax.all_to_all(out, "decode", 0, 0, axis_index_groups=PARITIES, tiled=True)
    other = project(1, rows, x_at, shards, w_at, before)
    own = project(0, rows, x_at, shards, w_at, after(before, other))
    queries, keys, values = rotate(own, to_d(other, CORE_SWAP), cosine, sine)

    def attend_chunk(chunk, queries):
        return attend(chunk, queries, cache_k[0, 0], cache_v[0, 0], keys, values, prefix_len)

    def spread(attended):
        return [attended] + [to_t(attended, pairs) for pairs in (X_UP, X_DOWN, X_FAR)]

    def back(partial):
        got = lax.all_to_all(partial, "tensor", 0, 0, tiled=True)
        return got.reshape(8, 32, partial.shape[1])

    own_rows, over_rows = page_rows(keys, values, page_owner)
    first = attend_chunk(0, queries)
    first_pieces = spread(first)
    second = attend_chunk(1, after(queries, first))
    second = after(second, *first_pieces[1:])
    out, over_rows = together(out, over_rows, second)[:2]
    pair = jnp.stack([own_rows, over_rows])
    low, high = to_d(pair, Y_UP), to_d(pair, Y_DOWN)
    out_weights = out, to_d(out, CORE_SWAP)
    first_pieces[0] = after(first_pieces[0], second)
    second_pieces = spread(second)
    first_partial = output(first_pieces, out_weights, x, core)
    first_partial, *second_pieces = together(first_partial, *second_pieces)
    first_back = back(first_partial)
    low, high = together(low, high, first_partial)[:2]
    far = to_d(low, Y_UP)
    second_partial = output(second_pieces, out_weights, x, core)
    far = after(far, second_partial)
    sources = [pair, low, high, far]
    sources += [to_d(a, CORE_SWAP) for a in sources]
    placed = place_pages(sources, page_owner.shape[1], zh, y, core, d)
    first_back = after(first_back, second_partial)
    second_back = back(after(second_partial, first_back))
    second_back = after(second_back, placed[0])
    attn_out = finish([first_back, second_back])[None]
    return (attn_out, *placed)


def solution(mesh):
    in_specs = (
        P("decode", "tensor", None),
        P(),
        P("decode", "tensor"),
        P("decode", "tensor"),
        P("decode", "tensor"),
        P("tensor", "decode"),
        P("decode", "tensor", None, None),
        P("decode", "tensor", None, None),
        P("decode"),
        P("decode", None),
    )
    out_specs = (
        P("decode", "tensor", None),
        P("decode", None, None, None, "tensor"),
        P("decode", None, None, "tensor"),
        P("decode", None),
    )
    return jax.shard_map(body, mesh=mesh, in_specs=in_specs, out_specs=out_specs, check_vma=False)
```

```python
import functools
import math

import jax
import jax.numpy as jnp
from jax import lax
from jax.experimental import pallas as pl
from jax.experimental.pallas import tpu as pltpu
from jax.sharding import PartitionSpec as P

CAP = 2
THETA = 500000.0
EPS = 1e-05
BF = jnp.bfloat16
F32 = jnp.float32
MB = 2**20


def tensor_perm(move):
    pairs = []
    for z in range(2):
        for x in range(4):
            a, b = move(z, x)
            pairs.append((z * 4 + x, a * 4 + b % 4))
    return pairs


def decode_perm(move):
    pairs = []
    for z in range(2):
        for y in range(4):
            for c in range(2):
                a, b, e = move(z, y, c)
                pairs.append((z * 8 + y * 2 + c, a * 8 + (b % 4) * 2 + e))
    return pairs


X_UP = tensor_perm(lambda z, x: (z, x + 1))
X_DOWN = tensor_perm(lambda z, x: (z, x - 1))
Z_SWAP = tensor_perm(lambda z, x: (1 - z, x))
Y_UP = decode_perm(lambda z, y, c: (z, y + 1, c))
Y_DOWN = decode_perm(lambda z, y, c: (z, y - 1, c))
Y_FAR = decode_perm(lambda z, y, c: (z, y + 2, c))
ZH_SWAP = decode_perm(lambda z, y, c: (1 - z, y, c))
CORE_SWAP = decode_perm(lambda z, y, c: (z, y, 1 - c))
PARITIES = [list(range(c, 16, 2)) for c in range(2)]
X_FAR = tensor_perm(lambda z, x: (z, x + 2))


def to_t(value, pairs):
    return lax.ppermute(value, "tensor", pairs)


def to_d(value, pairs):
    return lax.ppermute(value, "decode", pairs)


def after(value, *others):
    return lax.optimization_barrier((value, *others))[0]


def together(*values):
    return lax.optimization_barrier(values)


def gather_inputs(rows, w, w_at, out, tables):
    low, high = to_d(w, Y_UP), to_d(w, Y_DOWN)
    left, right, over = to_t(rows, X_UP), to_t(rows, X_DOWN), to_t(rows, Z_SWAP)
    low, high, left, right, over = together(low, high, left, right, over)
    w_over = to_d(after(w, low), ZH_SWAP)
    far_low = to_d(low, Y_UP)
    far = to_t(left, X_UP)
    over_right = to_t(over, X_DOWN)
    far, over_right, w_over, far_low, out, *tables = together(
        far, over_right, w_over, far_low, out, *tables
    )
    over_left = to_t(after(over, far), X_UP)
    over_far = to_t(over_right, X_DOWN)
    over_low, over_high = to_d(w_over, Y_UP), to_d(w_over, Y_DOWN)
    far_over = to_d(far_low, ZH_SWAP)
    early = [rows, left, right, far, over, over_right]
    here = [w, low, high, far_low]
    before = project_early(early, here, w_at)
    over_left, over_far, over_low, over_high, far_over, before, out = together(
        over_left, over_far, over_low, over_high, far_over, before, out
    )
    return (
        early + [over_left, over_far],
        here + [w_over, over_low, over_high, far_over],
        before,
        tables,
        out,
    )


def row_sources(z, x):
    here, there = z * 4, (1 - z) * 4
    lo, hi, end = (x + 3) % 4, (x + 1) % 4, (x + 2) % 4
    places = [here + at for at in (x, lo, hi, end)] + [there + at for at in (x, hi, lo, end)]
    return jnp.stack(places)


def shard_sources(zh, y):
    here, there = zh * 4, (1 - zh) * 4
    lo, hi, end = (y + 3) % 4, (y + 1) % 4, (y + 2) % 4
    return jnp.stack([first + at for first in (here, there) for at in (y, lo, hi, end)])


def stack_out(pieces, x):
    depth, wide = pieces[0].shape

    def kernel(x_ref, a0, a1, a2, a3, o_ref):
        for i, ref in enumerate((a0, a1, a2, a3)):
            to = pl.multiple_of((x_ref[0] + i) % 4 * depth, depth)
            for k in range(8):
                o_ref[k, pl.ds(to, depth), :] = ref[...]

    return pl.pallas_call(
        kernel,
        in_specs=[smem()] + [vmem()] * 4,
        out_specs=vmem(),
        out_shape=jax.ShapeDtypeStruct((8, 4 * depth, wide), BF),
        compiler_params=pltpu.CompilerParams(vmem_limit_bytes=20 * MB),
        name="stack",
    )(x[None].astype(jnp.int32), *pieces)


def hbm():
    return pl.BlockSpec(memory_space=pltpu.HBM)


def vmem():
    return pl.BlockSpec(memory_space=pltpu.VMEM)


def smem():
    return pl.BlockSpec(memory_space=pltpu.SMEM)


def prepare_kernel(at_ref, h_ref, gain_ref, wq, wk, wv, wo, keep_ref, send_ref, w_ref, *parts):
    q_cols, k_cols = wq.shape[1], wk.shape[1]
    w_ref[:, :q_cols] = wq[...]
    w_ref[:, q_cols : q_cols + k_cols] = wk[...]
    w_ref[:, q_cols + k_cols :] = wv[...]
    rows, width = h_ref.shape
    depth = wq.shape[0]
    even_core = at_ref[0] == 0
    wide = wo.shape[1] // 4
    for j, part in enumerate(parts):
        to = pl.multiple_of((at_ref[1] + j) % 4 * wide, wide)
        part[...] = wo[:, pl.ds(to, wide)]

    def step(i, carry):
        at = pl.ds(pl.multiple_of(i * 16, 16), 16)
        h = h_ref[at, :].astype(F32)
        mean_sq = jnp.sum(h * h, axis=1, keepdims=True) / width
        normed = (h * lax.rsqrt(mean_sq + EPS) * gain_ref[...]).astype(BF)
        for k in range(width // (2 * depth)):
            even = normed[:, 2 * k * depth : (2 * k + 1) * depth]
            odd = normed[:, (2 * k + 1) * depth : (2 * k + 2) * depth]
            keep_ref[at, k * depth : (k + 1) * depth] = jnp.where(even_core, even, odd)
            send_ref[at, k * depth : (k + 1) * depth] = jnp.where(even_core, odd, even)
        return carry

    lax.fori_loop(0, rows // 16, step, 0)


def prepare(hidden, gain, w_query, w_key, w_value, w_out, core, x):
    rows, width = hidden.shape
    depth = w_query.shape[0]
    cols = w_query.shape[1] + 2 * w_key.shape[1]
    return pl.pallas_call(
        prepare_kernel,
        in_specs=[smem()] + [vmem()] * 6,
        out_specs=[vmem()] * 7,
        out_shape=[
            jax.ShapeDtypeStruct((rows, width // 2), BF),
            jax.ShapeDtypeStruct((rows, width // 2), BF),
            jax.ShapeDtypeStruct((depth, cols), BF),
        ]
        + [jax.ShapeDtypeStruct((w_out.shape[0], w_out.shape[1] // 4), BF)] * 4,
        compiler_params=pltpu.CompilerParams(vmem_limit_bytes=60 * MB),
        name="prepare",
    )(jnp.stack([core, x]).astype(jnp.int32), hidden, gain[None], w_query, w_key, w_value, w_out)


def start_shards(refs, w_at, wv, sem):
    for i, ref in enumerate(refs):
        depth = ref.shape[0]
        to = pl.multiple_of(w_at[i] % 4 * depth, depth)
        pltpu.make_async_copy(ref, wv.at[pl.ds(to, depth), :], sem).start()


def project_early_kernel(w_at, *refs):
    xs, ws = refs[:6], refs[6:10]
    o_ref, xv, wv, xsem, wsem = refs[10:]
    rows, wide = xs[0].shape[0], xv.shape[1]
    columns = pl.ds(pl.multiple_of(w_at[0] // 4 * wide, wide), wide)
    for i, ref in enumerate(xs):
        to = xv.at[i * rows : (i + 1) * rows, :]
        pltpu.make_async_copy(ref.at[:, columns], to, xsem).start()
    start_shards(ws, w_at, wv, wsem)
    pltpu.make_async_copy(xv, xv, xsem).wait()
    pltpu.make_async_copy(wv, wv, wsem).wait()
    for n in range(o_ref.shape[1] // 256):
        at = slice(n * 256, n * 256 + 256)
        o_ref[:, at] = jnp.dot(xv[...], wv[:, at], preferred_element_type=F32)


def project_early(rows, shards, w_at):
    n = len(rows) * rows[0].shape[0]
    wide, cols = rows[0].shape[1] // 2, shards[0].shape[1]
    return pl.pallas_call(
        project_early_kernel,
        in_specs=[smem()] + [hbm()] * 10,
        out_specs=vmem(),
        out_shape=jax.ShapeDtypeStruct((n, cols), F32),
        scratch_shapes=[
            pltpu.VMEM((n, wide), BF),
            pltpu.VMEM((wide, cols), BF),
            pltpu.SemaphoreType.DMA,
            pltpu.SemaphoreType.DMA,
        ],
        compiler_params=pltpu.CompilerParams(vmem_limit_bytes=60 * MB),
        cost_estimate=pl.CostEstimate(flops=1, bytes_accessed=1, transcendentals=0),
        name="project_early",
    )(w_at, *rows, *shards)


def project_kernel(prompt, x_at, w_at, *refs):
    xs, ws, before = refs[:8], refs[8:16], refs[16]
    o_ref, there, here, bv, wt, wh, acc, sems = refs[17:]
    wide = there.shape[1]
    part = o_ref.shape[0] // 8
    mine = pl.ds(prompt * part, part)
    side = w_at[0] // 4
    here_columns = pl.ds(pl.multiple_of(side * wide, wide), wide)
    there_columns = pl.ds(pl.multiple_of((1 - side) * wide, wide), wide)
    for i, ref in enumerate(xs):
        to = there.at[i * part : (i + 1) * part, :]
        pltpu.make_async_copy(ref.at[mine, there_columns], to, sems.at[0]).start()
    for i, ref in enumerate(ws[4:]):
        depth = ref.shape[0]
        to = pl.multiple_of(w_at[4 + i] % 4 * depth, depth)
        pltpu.make_async_copy(ref, wt.at[pl.ds(to, depth), :], sems.at[1]).start()
    for i in range(6):
        to = bv.at[i * part : (i + 1) * part, :]
        source = before.at[i * 2 * part + prompt * part : i * 2 * part + (prompt + 1) * part, :]
        pltpu.make_async_copy(source, to, sems.at[2]).start()
    for i in range(2):
        to = here.at[i * part : (i + 1) * part, :]
        pltpu.make_async_copy(xs[6 + i].at[mine, here_columns], to, sems.at[3]).start()
    start_shards(ws[:4], w_at, wh, sems.at[4])
    pltpu.make_async_copy(there, there, sems.at[0]).wait()
    pltpu.make_async_copy(wt, wt, sems.at[1]).wait()
    cols = acc.shape[1]
    for n in range(cols // 256):
        at = slice(n * 256, n * 256 + 256)
        acc[:, at] = jnp.dot(there[...], wt[:, at], preferred_element_type=F32)
    pltpu.make_async_copy(bv, bv, sems.at[2]).wait()
    acc[: 6 * part, :] += bv[...]
    pltpu.make_async_copy(here, here, sems.at[3]).wait()
    pltpu.make_async_copy(wh, wh, sems.at[4]).wait()
    for n in range(cols // 256):
        at = slice(n * 256, n * 256 + 256)
        acc[6 * part :, at] += jnp.dot(here[...], wh[:, at], preferred_element_type=F32)
    for i in range(8):
        for r in range(2):
            to = pl.multiple_of(x_at[i] * 32 + r * (o_ref.shape[0] // 2), 32)
            o_ref[pl.ds(to, 32), :] = acc[i * part + r * 32 : i * part + r * 32 + 32, :]


def project(prompt, rows, x_at, shards, w_at, before):
    span, wide = rows[0].shape[0] * 4, rows[0].shape[1] // 2
    cols = shards[0].shape[1]
    return pl.pallas_call(
        functools.partial(project_kernel, prompt),
        in_specs=[smem()] * 2 + [hbm()] * 17,
        out_specs=vmem(),
        out_shape=jax.ShapeDtypeStruct((span, cols), F32),
        scratch_shapes=[
            pltpu.VMEM((span, wide), BF),
            pltpu.VMEM((span // 4, wide), BF),
            pltpu.VMEM((span // 4 * 3, cols), F32),
            pltpu.VMEM((wide, cols), BF),
            pltpu.VMEM((wide, cols), BF),
            pltpu.VMEM((span, cols), F32),
            pltpu.SemaphoreType.DMA((5,)),
        ],
        compiler_params=pltpu.CompilerParams(vmem_limit_bytes=60 * MB),
        cost_estimate=pl.CostEstimate(flops=1, bytes_accessed=1, transcendentals=0),
        name="project",
    )(x_at, w_at, *rows, *shards, before)


def rotate_kernel(rot_scale, a_ref, b_ref, cos_ref, sin_ref, q_ref, k_ref, v_ref):
    cos, sin = cos_ref[...], sin_ref[...]
    heads = q_ref.shape[0]

    def total(j):
        at = slice(j * 128, (j + 1) * 128)
        return a_ref[:, at] + b_ref[:, at]

    def rotated(j):
        part = total(j)
        return part * cos + pltpu.roll(part, 64, 1) * sin

    for j in range(heads):
        q_ref[j] = (rotated(j) * rot_scale).astype(BF)
    keys = rotated(heads).astype(BF)
    values = total(heads + 1).astype(BF)
    half = keys.shape[0] // 2
    for s in range(half // 32):
        for r in range(2):
            rows = slice(r * half + s * 32, r * half + s * 32 + 32)
            to = slice(s * 64 + r * 32, s * 64 + r * 32 + 32)
            k_ref[to, :] = keys[rows]
            v_ref[to, :] = values[rows]


def rotate(own, got, cosine, sine):
    span, cols = own.shape
    heads = cols // 128 - 2
    scale = math.log2(math.e) / math.sqrt(128)
    return pl.pallas_call(
        functools.partial(rotate_kernel, scale),
        in_specs=[vmem()] * 4,
        out_specs=[vmem()] * 3,
        out_shape=[
            jax.ShapeDtypeStruct((heads, span, 128), BF),
            jax.ShapeDtypeStruct((span, 128), BF),
            jax.ShapeDtypeStruct((span, 128), BF),
        ],
        compiler_params=pltpu.CompilerParams(vmem_limit_bytes=60 * MB),
        name="rotate",
    )(own, got, cosine, sine)


def attend_kernel(
    chunk, block, live_ref, q_ref, k_hbm, v_hbm, kn_ref, vn_ref, o_ref, k_ref, v_ref, sa, sb,
    total_ref, out_ref, sems
):
    heads, rows, width = q_ref.shape
    live = live_ref[0]
    blocks = k_ref.shape[0] // block
    q = q_ref[...].reshape(heads * rows, width)
    full = live // block
    left = live - full * block

    def loads(j):
        at = pl.ds(pl.multiple_of(j * block, block), block)
        return (
            pltpu.make_async_copy(k_hbm.at[at, :], k_ref.at[at, :], sems.at[0, j]),
            pltpu.make_async_copy(v_hbm.at[at, :], v_ref.at[at, :], sems.at[1, j]),
        )

    for j in range(blocks):
        for load in loads(j):
            load.start()

    def arrive(j):
        for load in loads(j):
            load.wait()

    def part(ref, j):
        return ref[pl.ds(pl.multiple_of(j * block, block), block), :]

    def scores(keys):
        return lax.dot_general(q, keys, (((1,), (1,)), ((), ())), preferred_element_type=F32)

    def lanes(values):
        return functools.reduce(
            jnp.add, [values[:, c * 128 : (c + 1) * 128] for c in range(values.shape[1] // 128)]
        )

    def weigh(s, top, values):
        p = jnp.exp2(s - top)
        return lanes(p), jnp.dot(p.astype(BF), values, preferred_element_type=F32)

    def add(s, top, values):
        more, term = weigh(s, top, values)
        total_ref[...] += more
        out_ref[...] += term

    def finish():
        r = (out_ref[...] / jnp.sum(total_ref[...], axis=1, keepdims=True)).astype(BF)
        for h in range(heads):
            o_ref[:, h * width : (h + 1) * width] = r[h * rows : (h + 1) * rows]

    def masked_part():
        s = scores(part(k_ref, full))
        return jnp.where(lax.broadcasted_iota(jnp.int32, s.shape, 1) < left, s, -1e30)

    def masked_new():
        s = scores(kn_ref[...])
        i = lax.broadcasted_iota(jnp.int32, s.shape, 0) % rows
        row = i // 32 * 64 + chunk * 32 + i % 32
        return jnp.where(lax.broadcasted_iota(jnp.int32, s.shape, 1) <= row, s, -1e30)

    arrive(0)
    sa[...] = scores(part(k_ref, 0))
    top = jnp.max(sa[...], axis=1, keepdims=True)
    total_ref[...] = jnp.zeros_like(total_ref)
    out_ref[...] = jnp.zeros_like(out_ref)

    def pair(i, carry):
        arrive(2 * i + 1)
        after = jnp.minimum(2 * i + 2, blocks - 1)

        @pl.when(2 * i + 2 < blocks)
        def _():
            arrive(2 * i + 2)

        sb[...] = scores(part(k_ref, 2 * i + 1))
        add(sa[...], top, part(v_ref, 2 * i))
        sa[...] = scores(part(k_ref, after))
        add(sb[...], top, part(v_ref, 2 * i + 1))
        return carry

    lax.fori_loop(0, full // 2, pair, 0)

    def rest(j, carry):
        arrive(j)
        return carry

    lax.fori_loop(full // 2 * 2 + 1, blocks, rest, 0)

    @pl.when(full % 2 == 1)
    def _():
        add(sa[...], top, part(v_ref, full - 1))

    @pl.when(left > 0)
    def _():
        add(masked_part(), top, part(v_ref, full))

    add(masked_new(), top, vn_ref[...])
    finish()

    @pl.when(jnp.max(total_ref[...]) > 2.0**40)
    def _():
        def running(top, s, values):
            new_top = jnp.maximum(top, jnp.max(s, axis=1, keepdims=True))
            keep = jnp.exp2(top - new_top)
            more, term = weigh(s, new_top, values)
            total_ref[...] = total_ref[...] * keep + more
            out_ref[...] = out_ref[...] * keep + term
            return new_top

        total_ref[...] = jnp.zeros_like(total_ref)
        out_ref[...] = jnp.zeros_like(out_ref)

        def body(j, top):
            return running(top, scores(part(k_ref, j)), part(v_ref, j))

        top_now = lax.fori_loop(0, full, body, top)
        top_now = lax.cond(
            left > 0, lambda t: running(t, masked_part(), part(v_ref, full)), lambda t: t, top_now
        )
        running(top_now, masked_new(), vn_ref[...])
        finish()

def attend(chunk, q, cache_k, cache_v, keys, values, live):
    heads, span, width = q.shape
    rows = span // 2
    prefix = cache_k.shape[0]
    block = 1024
    return pl.pallas_call(
        functools.partial(attend_kernel, chunk, block),
        grid=(1,),
        in_specs=[
            smem(),
            pl.BlockSpec((heads, rows, width), lambda i: (0, chunk, 0)),
            hbm(),
            hbm(),
            vmem(),
            vmem(),
        ],
        out_specs=pl.BlockSpec((rows, heads * width), lambda i: (0, 0)),
        out_shape=jax.ShapeDtypeStruct((rows, heads * width), BF),
        scratch_shapes=[
            pltpu.VMEM((prefix, width), BF),
            pltpu.VMEM((prefix, width), BF),
            pltpu.VMEM((heads * rows, block), F32),
            pltpu.VMEM((heads * rows, block), F32),
            pltpu.VMEM((heads * rows, 128), F32),
            pltpu.VMEM((heads * rows, width), F32),
            pltpu.SemaphoreType.DMA((2, prefix // block)),
        ],
        compiler_params=pltpu.CompilerParams(vmem_limit_bytes=60 * MB),
        cost_estimate=pl.CostEstimate(flops=1, bytes_accessed=1, transcendentals=0),
        name="attend",
    )(live, q, cache_k, cache_v, keys, values)


def output_kernel(x_at, a0, a1, a2, a3, mine, other, o_ref, xv, wv, xsem, wsem):
    shards, depth, cols = wv.shape
    core = x_at[4]
    width = a0.shape[1]
    copies = []
    for i, ref in enumerate((a0, a1, a2, a3)):
        to = pl.multiple_of(x_at[i] * width, width)
        copies.append(pltpu.make_async_copy(ref, xv.at[:, pl.ds(to, width)], xsem.at[i]))
    for copy in copies:
        copy.start()
    for k in range(shards // 2):
        sem = wsem.at[k // 2]
        pltpu.make_async_copy(mine.at[k], wv.at[2 * k + core], sem).start()
        pltpu.make_async_copy(other.at[k], wv.at[2 * k + 1 - core], sem).start()
    for copy in copies:
        copy.wait()
    for i in range(shards // 4):
        group = wv.at[4 * i : 4 * i + 4]
        pltpu.make_async_copy(group, group, wsem.at[i]).wait()
        w = jnp.concatenate([wv[j] for j in range(4 * i, 4 * i + 4)], axis=1)
        o_ref[:, 4 * i * cols : 4 * (i + 1) * cols] = jnp.dot(
            xv[...], w, preferred_element_type=F32
        ).astype(BF)


def output(pieces, weights, x, core):
    rows, width = pieces[0].shape
    x_at = jnp.stack([x, (x + 3) % 4, (x + 1) % 4, (x + 2) % 4, core]).astype(jnp.int32)
    shards, depth, cols = weights[0].shape
    shards = 2 * shards
    return pl.pallas_call(
        output_kernel,
        in_specs=[smem()] + [hbm()] * 6,
        out_specs=vmem(),
        out_shape=jax.ShapeDtypeStruct((rows, shards * cols), BF),
        scratch_shapes=[
            pltpu.VMEM((rows, 4 * width), BF),
            pltpu.VMEM((shards, depth, cols), BF),
            pltpu.SemaphoreType.DMA((4,)),
            pltpu.SemaphoreType.DMA((4,)),
        ],
        compiler_params=pltpu.CompilerParams(vmem_limit_bytes=60 * MB),
        cost_estimate=pl.CostEstimate(flops=1, bytes_accessed=1, transcendentals=0),
        name="output",
    )(x_at, *pieces, *weights)


def finish_kernel(*refs):
    o_ref = refs[-1]
    for r, ref in enumerate(refs[:-1]):
        for x in range(4):
            total = ref[x].astype(F32) + ref[4 + x].astype(F32)
            total = total.astype(BF)
            for d in range(16):
                to = d * 512 + x * 128
                o_ref[r * 32 : r * 32 + 32, to : to + 128] = total[:, d * 128 : d * 128 + 128]


def finish(parts):
    rows = parts[0].shape[1] * len(parts)
    return pl.pallas_call(
        finish_kernel,
        in_specs=[vmem()] * len(parts),
        out_specs=vmem(),
        out_shape=jax.ShapeDtypeStruct((rows, parts[0].shape[2] * 4), BF),
        compiler_params=pltpu.CompilerParams(vmem_limit_bytes=60 * MB),
        name="finish",
    )(*parts)


def place_kernel(page_of, at_ref, *refs):
    sources, (out_ref, scale_ref) = refs[:8], refs[8:]
    page = out_ref.shape[2]

    def slot(s, carry):
        number = page_of[s]
        prompt = s // CAP
        away = (prompt // 2 + 4 - at_ref[1]) % 4
        piece = jnp.where(away == 3, 1, jnp.where(away == 0, 0, away + 1))
        side = (prompt // 8 != at_ref[0]).astype(jnp.int32)
        source = piece + 4 * (prompt % 2 != at_ref[2]).astype(jnp.int32)

        @pl.when(number < 0)
        def _():
            out_ref[s] = jnp.zeros(out_ref.shape[1:], BF)
            scale_ref[s] = jnp.zeros(scale_ref.shape[1:], F32)

        for i, ref in enumerate(sources):

            @pl.when((number >= 0) & (source == i))
            def _(ref=ref):
                at = pl.multiple_of(jnp.maximum(number, 0) * page, page)
                rows = ref[side, pl.ds(at, page), :].astype(F32)
                for c in range(2):
                    part = rows[:, c * 128 : (c + 1) * 128]
                    most = jnp.max(jnp.abs(part), axis=0, keepdims=True)
                    most = jnp.max(most, axis=1, keepdims=True)
                    scale = (most + 1e-06).astype(BF).astype(F32)
                    out_ref[s, c] = (part / scale).astype(BF)
                    scale_ref[s, c : c + 1, :] = jnp.broadcast_to(scale, (1, 128))

        return carry

    lax.fori_loop(0, out_ref.shape[0], slot, 0)


def page_rows(keys, values, page_owner):
    count = page_owner.shape[1]
    marks = jnp.pad(page_owner.astype(BF), ((0, 15), (0, 256 - count)))
    own = jnp.concatenate([jnp.concatenate([keys, values], axis=1), marks], axis=0)
    return own, to_d(own, ZH_SWAP)


def marks_kernel(*refs):
    sources, o_ref, sems = refs[:8], refs[8], refs[9]
    rows = o_ref.shape[2]
    copies = []
    for i, ref in enumerate(sources):
        last = ref.at[:, pl.ds(ref.shape[1] - rows, rows), :]
        copies.append(pltpu.make_async_copy(last, o_ref.at[i], sems.at[i]))
    for copy in copies:
        copy.start()
    for copy in copies:
        copy.wait()


def owner_marks(sources):
    sides, _, width = sources[0].shape
    return pl.pallas_call(
        marks_kernel,
        in_specs=[hbm()] * 8,
        out_specs=vmem(),
        out_shape=jax.ShapeDtypeStruct((8, sides, 16, width), BF),
        scratch_shapes=[pltpu.SemaphoreType.DMA((8,))],
        compiler_params=pltpu.CompilerParams(vmem_limit_bytes=60 * MB),
        cost_estimate=pl.CostEstimate(flops=1, bytes_accessed=1, transcendentals=0),
        name="marks",
    )(*sources)


def place_pages(sources, count, zh, y, core, d):
    span = sources[0].shape[1] - 16
    order = jnp.arange(count, dtype=jnp.int32)
    prompt = jnp.arange(16)
    away = (prompt // 2 - y) % 4
    piece = jnp.array([0, 2, 3, 1])[away]
    source = piece + 4 * (prompt % 2 != core)
    side = (prompt // 8 != zh).astype(jnp.int32)
    marks = owner_marks(sources)[:, :, 0, :count].reshape(16, count).astype(F32)
    pick = (source * 2 + side)[:, None] == jnp.arange(16)[None, :]
    owners = jnp.sum(jnp.where(pick[:, :, None], marks[None], 0.0), axis=1).astype(jnp.int32)
    same = owners[:, :, None] == owners[:, None, :]
    rank = jnp.sum((same & (order[None, :] < order[:, None])[None]).astype(jnp.int32), axis=2)
    chosen = (owners == d)[:, None, :] & (rank[:, None, :] == jnp.arange(CAP)[None, :, None])
    ids = jnp.max(jnp.where(chosen, order[None, None, :], -1), axis=2).reshape(16 * CAP)
    pages, scales = pl.pallas_call(
        place_kernel,
        in_specs=[smem(), smem()] + [vmem()] * 8,
        out_specs=[vmem()] * 2,
        out_shape=[
            jax.ShapeDtypeStruct((16 * CAP, 2, span // count, 128), BF),
            jax.ShapeDtypeStruct((16 * CAP, 2, 128), F32),
        ],
        compiler_params=pltpu.CompilerParams(vmem_limit_bytes=60 * MB),
        cost_estimate=pl.CostEstimate(flops=1, bytes_accessed=1, transcendentals=0),
        name="place",
    )(ids, jnp.stack([zh, y, core]).astype(jnp.int32), *sources)
    return pages[None], scales[None, :, :, :1].astype(BF), ids[None]


def rope_tables(positions, width):
    half = width // 2
    steps = jnp.arange(half, dtype=F32) * (2.0 / width)
    freqs = jnp.exp(-math.log(THETA) * steps)
    angles = positions.astype(F32)[:, None] * freqs[None, :]
    cosine, sine = jnp.cos(angles), jnp.sin(angles)
    return (
        jnp.concatenate([cosine, cosine], axis=1),
        jnp.concatenate([-sine, sine], axis=1),
    )


def body(
    hidden_in, norm_gain, w_query, w_key, w_value, w_out, cache_k, cache_v, prefix_len, page_owner
):
    t, d = lax.axis_index("tensor"), lax.axis_index("decode")
    z, x = t // 4, t % 4
    zh, y, core = d // 8, d // 2 % 4, d % 2
    span = hidden_in.shape[1] * 8
    width = cache_k.shape[-1]
    i = jnp.arange(span, dtype=jnp.int32)
    true_row = i % (span // 2) // 32 * 64 + i // (span // 2) * 32 + i % 32
    tables = rope_tables(prefix_len[0] + true_row, width)
    keep, send, w, *quarters = prepare(
        hidden_in[0], norm_gain, w_query, w_key, w_value, w_out, core, x
    )
    moves = (X_UP, X_FAR, X_DOWN)
    quarters = [quarters[0]] + [to_t(a, pairs) for a, pairs in zip(quarters[1:], moves)]
    chip_rows = jnp.concatenate([keep, to_d(send, CORE_SWAP)], axis=0)
    chip_rows, *quarters = together(chip_rows, *quarters)
    out = stack_out([quarters[i] for i in (0, 3, 2, 1)], x)
    x_at = row_sources(z, x).astype(jnp.int32)
    w_at = shard_sources(zh, y).astype(jnp.int32)
    rows, shards, before, (cosine, sine), out = gather_inputs(chip_rows, w, w_at, out, tables)
    out = lax.all_to_all(out, "decode", 0, 0, axis_index_groups=PARITIES, tiled=True)
    other = project(1, rows, x_at, shards, w_at, before)
    own = project(0, rows, x_at, shards, w_at, after(before, other))
    queries, keys, values = rotate(own, to_d(other, CORE_SWAP), cosine, sine)

    def attend_chunk(chunk, queries):
        return attend(chunk, queries, cache_k[0, 0], cache_v[0, 0], keys, values, prefix_len)

    def spread(attended):
        return [attended] + [to_t(attended, pairs) for pairs in (X_UP, X_DOWN, X_FAR)]

    def back(partial):
        got = lax.all_to_all(partial, "tensor", 0, 0, tiled=True)
        return got.reshape(8, 32, partial.shape[1])

    own_rows, over_rows = page_rows(keys, values, page_owner)
    first = attend_chunk(0, queries)
    first_pieces = spread(first)
    second = attend_chunk(1, after(queries, first))
    second = after(second, *first_pieces[1:])
    out, over_rows = together(out, over_rows, second)[:2]
    pair = jnp.stack([own_rows, over_rows])
    low, high = to_d(pair, Y_UP), to_d(pair, Y_DOWN)
    out_weights = out, to_d(out, CORE_SWAP)
    first_pieces[0] = after(first_pieces[0], second)
    second_pieces = spread(second)
    first_partial = output(first_pieces, out_weights, x, core)
    first_partial, *second_pieces = together(first_partial, *second_pieces)
    first_back = back(first_partial)
    low, high = together(low, high, first_partial)[:2]
    far = to_d(low, Y_UP)
    second_partial = output(second_pieces, out_weights, x, core)
    far = after(far, second_partial)
    sources = [pair, low, high, far]
    sources += [to_d(a, CORE_SWAP) for a in sources]
    placed = place_pages(sources, page_owner.shape[1], zh, y, core, d)
    first_back = after(first_back, second_partial)
    second_back = back(after(second_partial, first_back))
    second_back = after(second_back, placed[0])
    attn_out = finish([first_back, second_back])[None]
    return (attn_out, *placed)


def solution(mesh):
    in_specs = (
        P("decode", "tensor", None),
        P(),
        P("decode", "tensor"),
        P("decode", "tensor"),
        P("decode", "tensor"),
        P("tensor", "decode"),
        P("decode", "tensor", None, None),
        P("decode", "tensor", None, None),
        P("decode"),
        P("decode", None),
    )
    out_specs = (
        P("decode", "tensor", None),
        P("decode", None, None, None, "tensor"),
        P("decode", None, None, "tensor"),
        P("decode", None),
    )
    return jax.shard_map(body, mesh=mesh, in_specs=in_specs, out_specs=out_specs, check_vma=False)
```
